256 devices in a mesh: rx: 8 (over x, core), ry: 32 (over y, z).
Axes of the slice: x: 4, y: 4, z: 8, core: 2. Of those that a mesh axis runs over, the one named last changes fastest.
Arguments:
- rhs: float32 [2, 11, 64, 16384], P(None, None, 'rx', 'ry'), may hold values from -6 to 6
- viscosity: float32 [10, 2, 64, 16384], P(None, None, 'rx', 'ry'), may hold values from 0.2 to 4
- cell_mask: int32 [64, 16384], P('rx', 'ry'), may hold values 0 or 1
- friction: float32 [64, 16384], P('rx', 'ry'), may hold values from 0.1 to 10
- stiffness: float32 [2, 12, 12], replicated, may hold values from -1.75 to 1.75
Outputs:
- update: float32 [2, 11, 64, 16384], P(None, None, 'rx', 'ry')
- last_basis: float32 [2, 11, 64, 16384], P(None, None, 'rx', 'ry')
The draws below stay inside these ranges and needn't reach their ends.
All inputs are finite; a program needn't handle non-finite values. No bound on the sum of `cell_mask` on one device may be relied on, other than what follows from the above.
Results may differ from the reference program's by a relative error of at most 0.00012.
Values sent between devices are 32-bit elements; how exact they have to be, the bound alone decides.
No kernel may reach another device: no remote copies, remote signals or barrier semaphores. Data moves between devices by JAX's collectives and lax.ppermute only.
A program may use at most 64 MiB of HBM per device.

```python
import math
import jax
import jax.numpy as jnp
from jax import lax

NL = 10
ITERS = 3
NX = 64
NY = 16384


def place_ends(drawn, key, least, top_value):
    extent = drawn.shape
    spot = [jax.random.randint(jax.random.fold_in(key, axis), (), 0, extent[axis]) for axis in range(len(extent))]
    drawn = drawn.at[tuple(spot)].set(least)
    longest = extent.index(max(extent))
    spot[longest] = (spot[longest] + 1) % extent[longest]
    return drawn.at[tuple(spot)].set(top_value)


def block_levels(own_key, dims, split, least, largest):
    def one(position, shards_of):
        draws = jax.random.uniform(jax.random.fold_in(jax.random.fold_in(own_key, 6), position), (shards_of,), jnp.float32, least / len(split), largest / len(split))
        return jnp.repeat(jnp.exp(draws), dims[position] // shards_of).reshape((-1,) + (1,) * (len(dims) - position - 1))

    gain = one(*split[0])
    for cut in split[1:]:
        gain = gain * one(*cut)
    return gain


def centred(key, extent, scale, reach, split=(), kind=jnp.bfloat16):
    level = block_levels(key, extent, split, -0.22, 0.18) if split else 1.0
    values = jax.random.normal(key, extent, jnp.float32) * scale * level
    return jnp.minimum(jnp.maximum(values, -reach), reach).astype(kind)


def setup_inputs(seed: int = 0) -> dict:
    splits = jax.random.split(jax.random.key(seed), 6)
    rhs = centred(splits[0], (2, NL + 1, NX, NY), 1.0, 6.0, ((2, 8), (3, 32)), jnp.float32)
    viscosity = jnp.clip(jnp.exp(math.log(4.0) - 2.9957323 * jax.random.uniform(splits[1], (NL, 2, NX, NY), jnp.float32) ** block_levels(splits[1], (NL, 2, NX, NY), ((2, 8), (3, 32)), -0.2, 0.2)), 0.2, 4.0)
    cell_mask = place_ends((jax.random.randint(splits[2], (NX, NY), 0, 8) < 7).astype(jnp.int32), jax.random.fold_in(splits[2], 1), 0, 1)
    friction = jnp.clip(jnp.exp(math.log(10.0) - 4.6051702 * jax.random.uniform(splits[3], (NX, NY), jnp.float32) ** block_levels(splits[3], (NX, NY), ((0, 8), (1, 32)), -0.2, 0.2)), 0.1, 10.0)
    stiffness = centred(splits[4], (2, 12, 12), 12 ** -0.5, 1.75, (), jnp.float32)
    return {"rhs": rhs, "viscosity": viscosity, "cell_mask": cell_mask, "friction": friction, "stiffness": stiffness}


OFFSETS = ((0, 0), (1, 0), (0, 1), (1, 1))
TRIANGLES = ((0, 1, 2), (1, 3, 2))

def element_apply(nodes, coef, stiff):
    rows = coef.shape[2]
    cols = coef.shape[3]
    layers = coef.shape[0]
    corners = [nodes[:, :, oi:oi + rows, oj:oj + cols] for oi, oj in OFFSETS]
    result = jnp.zeros_like(nodes)
    for tri in range(2):
        trio = TRIANGLES[tri]
        stacked = jnp.stack([corners[k] for k in trio], axis=0)
        levels = jnp.stack([stacked[:, :, :-1], stacked[:, :, 1:]], axis=0)
        local = jnp.transpose(levels, (2, 0, 1, 3, 4, 5)).reshape(12, layers, rows, cols)
        mixed = jnp.einsum('pq,qlrc->plrc', stiff[tri], local, precision=lax.Precision.HIGHEST)
        mixed = (mixed * coef[:, tri][None]).reshape(2, 2, 3, layers, rows, cols)
        for slot in range(3):
            node_part = jnp.pad(mixed[:, 0, slot], ((0, 0), (0, 1), (0, 0), (0, 0)))
            node_part = node_part + jnp.pad(mixed[:, 1, slot], ((0, 0), (1, 0), (0, 0), (0, 0)))
            shift_i, shift_j = OFFSETS[trio[slot]]
            result = result + jnp.pad(node_part, ((0, 0), (0, 0), (shift_i, 1 - shift_i), (shift_j, 1 - shift_j)))
    return result

def basal(field, friction):
    bottom = (friction[None] * field[:, 0])[:, None]
    return jnp.concatenate([bottom, jnp.zeros_like(field[:, 1:])], axis=1)

def least_squares(hess, norm0):
    count = len(hess[0])
    table = [list(line) for line in hess]
    target = [norm0] + [norm0 * 0.0 for step in range(count)]
    rotations = []
    for col in range(count):
        for row in range(col):
            cosine, sine = rotations[row]
            upper, lower = (table[row][col], table[row + 1][col])
            table[row][col] = cosine * upper + sine * lower
            table[row + 1][col] = cosine * lower - sine * upper
        first, second = (table[col][col], table[col + 1][col])
        radius = jnp.sqrt(first * first + second * second)
        cosine, sine = (first / radius, second / radius)
        rotations.append((cosine, sine))
        table[col][col] = radius
        upper, lower = (target[col], target[col + 1])
        target[col] = cosine * upper + sine * lower
        target[col + 1] = cosine * lower - sine * upper
    solved = [None] * count
    for col in range(count - 1, -1, -1):
        total = target[col]
        for later in range(col + 1, count):
            total = total - table[col][later] * solved[later]
        solved[col] = total / table[col][col]
    return solved

def reference(rhs, viscosity, cell_mask, friction, stiffness):
    coef = viscosity * cell_mask.astype(viscosity.dtype)[None, None]

    def operate(field):
        padded = jnp.pad(field, ((0, 0), (0, 0), (0, 1), (0, 1)))
        assembled = element_apply(padded, coef, stiffness)[:, :, :-1, :-1]
        return assembled + field + basal(field, friction)
    norm0 = jnp.sqrt(jnp.sum(rhs * rhs))
    basis = [rhs / norm0]
    hess = [[norm0 * 0.0 for col in range(ITERS)] for row in range(ITERS + 1)]
    for col in range(ITERS):
        work = operate(basis[col])
        dots = [jnp.sum(work * vector) for vector in basis]
        for row in range(col + 1):
            work = work - dots[row] * basis[row]
            hess[row][col] = dots[row]
        length = jnp.sqrt(jnp.sum(work * work))
        hess[col + 1][col] = length
        basis.append(work / length)
    solved = least_squares(hess, norm0)
    update = solved[0] * basis[0]
    for col in range(1, ITERS):
        update = update + solved[col] * basis[col]
    return (update, basis[ITERS])
```

```python
import functools

import jax
import jax.numpy as jnp
from jax import lax
from jax.experimental import pallas as pl
from jax.experimental.pallas import tpu as pltpu
from jax.sharding import PartitionSpec as P


DEPTH = 3
NROW = 8 + 2 * DEPTH
LANES = 640
HALF = 80
BLOCK = 2 * HALF
GROUPS = 144
VMEM_LIMIT = 56 * 1024 * 1024


def shift_of(stiff):
    rows = lax.broadcasted_iota(jnp.int32, (12, 12), 0)
    cols = lax.broadcasted_iota(jnp.int32, (12, 12), 1)
    trace = jnp.sum(jnp.where(rows == cols, stiff[0] + stiff[1], 0.0))
    return 1.0 + trace * (1.2 * 10.0 / 22.0)


def own_row(out, rhs, visc, mask, fric, row):
    ice = mask[row : row + 1, :].astype(jnp.float32)
    out[0:22, 0:512] = rhs[:, row, :]
    out[22:23, 0:512] = jnp.ones_like(ice)
    out[23:24, 0:512] = fric[row : row + 1, :]
    out[24:34, 0:512] = visc[:, 0, row, :] * ice
    out[34:44, 0:512] = visc[:, 1, row, :] * ice
    out[44:48, 0:512] = jnp.zeros((4, 512), jnp.float32)


def rows_kernel(rhs, visc, mask, fric, up, down):
    for j in range(DEPTH):
        own_row(up.at[j], rhs, visc, mask, fric, 8 - DEPTH + j)
        own_row(down.at[j], rhs, visc, mask, fric, j)


def cols_kernel(rhs, visc, mask, fric, low, high, right, left, work):
    lane = lax.broadcasted_iota(jnp.int32, (48, 128), 1)
    to_right = jnp.zeros((48, 128), jnp.float32)
    to_left = jnp.zeros((48, 128), jnp.float32)
    for i in range(NROW):
        if i < DEPTH:
            row = low.at[i]
        elif i >= 8 + DEPTH:
            row = high.at[i - 8 - DEPTH]
        else:
            own_row(work, rhs, visc, mask, fric, i - DEPTH)
            row = work
        here = (lane >= 8 * i) & (lane < 8 * i + DEPTH)
        first = row[:, 0:128]
        last = row[:, 384:512]
        to_right = jnp.where(here, pltpu.roll(last, (8 * i + DEPTH) % 128, 1), to_right)
        to_left = jnp.where(here, pltpu.roll(first, 8 * i, 1) if i else first, to_left)
    right[...] = to_right
    left[...] = to_left


def weights_kernel(stiff, weights):
    row = lax.broadcasted_iota(jnp.int32, (GROUPS, 12), 0)
    col = lax.broadcasted_iota(jnp.int32, (GROUPS, 12), 1)

    def of_row(r):
        group, plane = (r // 24, r % 24)
        slot, lev = (group // 2, group % 2)
        comp, level = (plane // 11, plane % 11)
        layer = level - lev
        good = (plane < 22) & (layer >= 0) & (layer < 10)
        return comp * 6 + lev * 3 + slot, layer, good

    pick = jnp.where(of_row(row)[0] == col, 1.0, 0.0)
    r = lax.broadcasted_iota(jnp.int32, (GROUPS, 3 * HALF), 0)
    k = lax.broadcasted_iota(jnp.int32, (GROUPS, 3 * HALF), 1)
    _, layer, good = of_row(r)
    part = (k % HALF) // 24
    plane = (k % HALF) % 24
    lev_in = plane % 11 - layer
    good = good & (part < 3) & (plane < 22)
    q = lax.broadcasted_iota(jnp.int32, (12, 3 * HALF), 0)
    kq = lax.broadcasted_iota(jnp.int32, (12, 3 * HALF), 1)
    comp_in = ((kq % HALF) % 24) // 11
    block = kq // HALF
    for tri in range(2):
        first, second, third = ((0, 2, 1), (2, 0, 1))[tri]
        place = jnp.where(block == 0, first, jnp.where(block == 1, second, third))
        rows = jnp.dot(
            pick, stiff[tri], precision=lax.Precision.HIGHEST, preferred_element_type=jnp.float32
        )
        total = jnp.zeros((GROUPS, 3 * HALF), jnp.float32)
        for lev in range(2):
            sel = jnp.where(comp_in * 6 + lev * 3 + place == q, 1.0, 0.0)
            spread = jnp.dot(
                rows, sel, precision=lax.Precision.HIGHEST, preferred_element_type=jnp.float32
            )
            total = jnp.where(good & (lev_in == lev), spread, total)
        high = total.astype(jnp.bfloat16).astype(jnp.float32)
        weights[tri] = jnp.where(part == 2, total - high, high).astype(jnp.bfloat16)


def split_rows(x):
    high = x.astype(jnp.bfloat16).astype(jnp.float32)
    pad = jnp.zeros((HALF - 72, x.shape[1]), jnp.float32)
    return jnp.concatenate([high, x - high, high, pad], axis=0).astype(jnp.bfloat16)


def put_operand(operand, i, x):
    start = pl.multiple_of(i * BLOCK, BLOCK)
    operand[pl.ds(start, HALF), :] = split_rows(x)
    operand[pl.ds(start + HALF, HALF), :] = split_rows(pltpu.roll(x, LANES - 1, 1))


def main_kernel(
    rhs, visc, mask, fric, low, high, from_left, from_right, stiff, weights,
    powers, gram,
    full, scale, diag, field, operand, carry,
):
    lane = lax.broadcasted_iota(jnp.int32, (48, 128), 1)
    theta = shift_of(stiff)
    plane = lax.broadcasted_iota(jnp.int32, (24, LANES), 0)
    bottom = (plane == 0) | (plane == 11)
    for i in range(NROW):
        row = full.at[i]
        if i < DEPTH:
            row[:, 0:512] = low[i]
        elif i >= 8 + DEPTH:
            row[:, 0:512] = high[i - 8 - DEPTH]
        else:
            own_row(row, rhs, visc, mask, fric, i - DEPTH)
        on_right = from_right[...]
        on_right = pltpu.roll(on_right, 128 - 8 * i, 1) if i else on_right
        on_left = pltpu.roll(from_left[...], (128 - DEPTH - 8 * i) % 128, 1)
        row[:, 512:640] = jnp.where(
            lane < DEPTH, on_right, jnp.where(lane >= 128 - DEPTH, on_left, 0.0)
        )
        real = row[22:23, :]
        x = jnp.where(plane < 22, row[0:24, :], 0.0)
        field[0, i] = x
        put_operand(operand.at[0], i, x)
        diag[i] = real * (1.0 - theta) + jnp.where(bottom, row[23:24, :], 0.0)
        if i < NROW - 1:
            for tri in range(2):
                coef = row[24 + 10 * tri : 34 + 10 * tri, :]
                for lev in range(2):
                    base = 48 * tri + 24 * lev
                    out = scale.at[i]
                    out[base : base + 24, :] = jnp.zeros((24, LANES), jnp.float32)
                    out[base + lev : base + lev + 10, :] = coef
                    out[base + 11 + lev : base + 21 + lev, :] = coef

    for step in range(1, DEPTH + 1):
        source = operand.at[(step - 1) % 2]
        target = operand.at[step % 2]
        carry[...] = jnp.zeros_like(carry)

        def cell_row(i, _, step=step, source=source, target=target):
            start = pl.multiple_of(i * BLOCK, BLOCK)
            mixed = [
                jnp.dot(
                    weights[tri],
                    source[pl.ds(start + HALF * tri, 3 * HALF), :],
                    preferred_element_type=jnp.float32,
                )
                for tri in range(2)
            ]
            grown = []
            for tri in range(2):
                upper = scale[i, 48 * tri : 48 * tri + 24, :]
                lower = scale[i, 48 * tri + 24 : 48 * tri + 48, :]
                for slot in range(3):
                    at = 48 * slot
                    grown.append(
                        upper * mixed[tri][at : at + 24] + lower * mixed[tri][at + 24 : at + 48]
                    )
            near = grown[0] + carry[0]
            far = grown[2] + grown[5] + carry[1]
            carry[0] = grown[1] + grown[3]
            carry[1] = grown[4]
            total = near + pltpu.roll(far, 1, 1)
            x = full[i, 22:23, :] * total + diag[i] * field[step - 1, i]
            field[step, i] = x
            if step < DEPTH:
                put_operand(target, i, x)
            return 0

        lax.fori_loop(step - 1, NROW - step, cell_row, 0)

    pairs = [(a, b) for a in range(4) for b in range(a, 4)]

    def add_row(r, sums):
        vectors = [field[a, r + DEPTH, :, 0:512] for a in range(4)]
        result = []
        for total, (a, b) in zip(sums, pairs):
            product = vectors[a] * vectors[b]
            for s in range(3):
                for l in range(4):
                    total = total + product[8 * s : 8 * s + 8, 128 * l : 128 * l + 128]
            result.append(total)
        for a in range(1, 4):
            powers[a - 1, r] = vectors[a]
        return tuple(result)

    sums = lax.fori_loop(
        0, 8, add_row, tuple(jnp.zeros((8, 128), jnp.float32) for _ in pairs)
    )
    place = lax.broadcasted_iota(jnp.int32, (8, 128), 1)
    line = jnp.zeros((8, 128), jnp.float32)
    for n, total in enumerate(sums):
        line = jnp.where(place == n, jnp.sum(total), line)
    devices = gram.shape[0]
    gram[...] = jnp.broadcast_to(line[0:1], (devices, 128))


def combine_kernel(rhs, powers, grams, stiff, update, last):
    theta = shift_of(stiff)
    entry = jnp.sum(grams[...], axis=0, keepdims=True)
    place = lax.broadcasted_iota(jnp.int32, (1, 128), 1)
    pairs = [(a, b) for a in range(4) for b in range(a, 4)]
    g = {}
    for n, pair in enumerate(pairs):
        g[pair] = jnp.sum(jnp.where(place == n, entry, 0.0), axis=1, keepdims=True)
    upper = [[None] * 4 for _ in range(4)]
    for a in range(4):
        for b in range(a, 4):
            value = g[a, b]
            for c in range(a):
                value = value - upper[c][a] * upper[c][b]
            if a == b:
                upper[a][a] = jnp.sqrt(value)
            else:
                upper[a][b] = value / upper[a][a]
    zero = jnp.zeros((1, 1), jnp.float32)
    table = [
        [
            (upper[a][b + 1] if a <= b + 1 else zero) + (theta * upper[a][b] if a <= b else zero)
            for b in range(3)
        ]
        for a in range(4)
    ]
    target = [upper[0][0], zero, zero, zero]
    for col in range(3):
        first, second = (table[col][col], table[col + 1][col])
        radius = jnp.sqrt(first * first + second * second)
        cosine, sine = (first / radius, second / radius)
        for c in range(col, 3):
            one, two = (table[col][c], table[col + 1][c])
            table[col][c] = cosine * one + sine * two
            table[col + 1][c] = cosine * two - sine * one
        one, two = (target[col], target[col + 1])
        target[col] = cosine * one + sine * two
        target[col + 1] = cosine * two - sine * one
    z = [None] * 3
    for col in (2, 1, 0):
        value = target[col]
        for c in range(col + 1, 3):
            value = value - table[col][c] * z[c]
        z[col] = value / table[col][col]
    w = [None] * 4
    w[3] = 1.0 / upper[3][3]
    for a in (2, 1, 0):
        value = zero
        for c in range(a + 1, 4):
            value = value - upper[a][c] * w[c]
        w[a] = value / upper[a][a]
    for r in range(8):
        one = rhs[:, r, :]
        rest = [powers[a, r, 0:22, :] for a in range(3)]
        update[:, r, :] = z[0] * one + z[1] * rest[0] + z[2] * rest[1]
        last[:, r, :] = w[0] * one + w[1] * rest[0] + w[2] * rest[1] + w[3] * rest[2]


def call(kernel, outs, scratch=(), flops=0, bytes_accessed=0):
    single = not isinstance(outs, (list, tuple))
    return pl.pallas_call(
        kernel,
        out_shape=outs if single else tuple(outs),
        scratch_shapes=list(scratch),
        compiler_params=pltpu.CompilerParams(vmem_limit_bytes=VMEM_LIMIT),
        cost_estimate=pl.CostEstimate(
            flops=flops, bytes_accessed=bytes_accessed, transcendentals=0
        ),
    )


def f32(*shape):
    return jax.ShapeDtypeStruct(shape, jnp.float32)


def passed_along(shard, axis, by):
    devices = lax.axis_size(axis)
    pairs = [(i, i + by) for i in range(devices) if 0 <= i + by < devices]
    return lax.ppermute(shard, axis, pairs)


def body(rhs, viscosity, cell_mask, friction, stiffness):
    devices = lax.axis_size("rx") * lax.axis_size("ry")
    field = rhs.reshape(22, 8, 512)
    local = (field, viscosity, cell_mask, friction)
    weights = call(
        weights_kernel, jax.ShapeDtypeStruct((2, GROUPS, 3 * HALF), jnp.bfloat16), flops=10**7, bytes_accessed=10**5
    )(stiffness)
    up, down = call(rows_kernel, (f32(DEPTH, 48, 512),) * 2, bytes_accessed=10**6)(*local)
    low = passed_along(up, "rx", 1)
    high = passed_along(down, "rx", -1)
    right, left = call(
        cols_kernel, (f32(48, 128),) * 2, [pltpu.VMEM((48, 512), jnp.float32)], bytes_accessed=10**6
    )(*local, low, high)
    from_left = passed_along(right, "ry", 1)
    from_right = passed_along(left, "ry", -1)
    powers, gram = call(
        main_kernel,
        (f32(3, 8, 24, 512), f32(devices, 128)),
        [
            pltpu.VMEM((NROW, 48, LANES), jnp.float32),
            pltpu.VMEM((NROW - 1, 96, LANES), jnp.float32),
            pltpu.VMEM((NROW, 24, LANES), jnp.float32),
            pltpu.VMEM((4, NROW, 24, LANES), jnp.float32),
            pltpu.VMEM((2, NROW * BLOCK, LANES), jnp.bfloat16),
            pltpu.VMEM((2, 24, LANES), jnp.float32),
        ],
        flops=3 * 10**9,
        bytes_accessed=3 * 10**6,
    )(*local, low, high, from_left, from_right, stiffness, weights)
    grams = lax.all_to_all(gram.reshape(devices, 1, 128), ("rx", "ry"), 0, 0)
    update, last = call(combine_kernel, (f32(22, 8, 512),) * 2, bytes_accessed=3 * 10**6)(
        field, powers, grams.reshape(devices, 128), stiffness
    )
    return update.reshape(2, 11, 8, 512), last.reshape(2, 11, 8, 512)


def solution(mesh):
    in_specs = (
        P(None, None, "rx", "ry"),
        P(None, None, "rx", "ry"),
        P("rx", "ry"),
        P("rx", "ry"),
        P(),
    )
    out_specs = (P(None, None, "rx", "ry"), P(None, None, "rx", "ry"))
    return jax.shard_map(body, mesh=mesh, in_specs=in_specs, out_specs=out_specs, check_vma=False)
```

```python
import jax
import jax.numpy as jnp
from jax import lax
from jax.experimental import pallas as pl
from jax.experimental.pallas import tpu as pltpu
from jax.sharding import PartitionSpec as P


DEPTH = 3
NROW = 8 + 2 * DEPTH
LANES = 640
HALF = 80
BLOCK = 2 * HALF
GROUPS = 144


def shift_of(stiff):
    rows = lax.broadcasted_iota(jnp.int32, (12, 12), 0)
    cols = lax.broadcasted_iota(jnp.int32, (12, 12), 1)
    trace = jnp.sum(jnp.where(rows == cols, stiff[0] + stiff[1], 0.0))
    return 1.0 + trace * (1.2 * 10.0 / 22.0)


def own_row(out, rhs, visc, mask, fric, row):
    ice = mask[row : row + 1, :].astype(jnp.float32)
    out[0:22, 0:512] = rhs[:, row, :]
    out[22:23, 0:512] = jnp.ones_like(ice)
    out[23:24, 0:512] = fric[row : row + 1, :]
    out[24:34, 0:512] = visc[:, 0, row, :] * ice
    out[34:44, 0:512] = visc[:, 1, row, :] * ice
    out[44:48, 0:512] = jnp.zeros((4, 512), jnp.float32)


def odd_along(axis):
    return lax.rem(lax.axis_index(axis), 2) == 1


def rows_kernel(rhs, visc, mask, fric, first, second, work):
    odd = odd_along("rx")
    for j in range(DEPTH):
        own_row(work.at[0], rhs, visc, mask, fric, 8 - DEPTH + j)
        own_row(work.at[1], rhs, visc, mask, fric, j)
        up, down = (work[0], work[1])
        first[j] = jnp.where(odd, down, up)
        second[j] = jnp.where(odd, up, down)


def pack_row(row, i, lane, packs):
    here = (lane >= 8 * i) & (lane < 8 * i + DEPTH)
    start, end = (row[:, 0:128], row[:, 384:512])
    to_right = jnp.where(here, pltpu.roll(end, (8 * i + DEPTH) % 128, 1), packs[0])
    to_left = jnp.where(here, pltpu.roll(start, 8 * i, 1) if i else start, packs[1])
    return to_right, to_left


def own_kernel(rhs, visc, mask, fric, stiff, own, packs, weights):
    weights_kernel(stiff, weights)
    lane = lax.broadcasted_iota(jnp.int32, (48, 128), 1)
    both = (jnp.zeros((48, 128), jnp.float32),) * 2
    for r in range(8):
        own_row(own.at[r], rhs, visc, mask, fric, r)
        both = pack_row(own.at[r], r + DEPTH, lane, both)
    packs[0], packs[1] = both


def cols_kernel(packs, first_rows, second_rows, first, second):
    odd_row = odd_along("rx")
    odd = odd_along("ry")
    lane = lax.broadcasted_iota(jnp.int32, (48, 128), 1)
    both = (packs[0], packs[1])
    for j in range(DEPTH):
        one, two = (first_rows[j], second_rows[j])
        both = pack_row(jnp.where(odd_row, one, two), j, lane, both)
        both = pack_row(jnp.where(odd_row, two, one), j + 8 + DEPTH, lane, both)
    first[...] = jnp.where(odd, both[1], both[0])
    second[...] = jnp.where(odd, both[0], both[1])


def weights_kernel(stiff, weights):
    row = lax.broadcasted_iota(jnp.int32, (GROUPS, 12), 0)
    col = lax.broadcasted_iota(jnp.int32, (GROUPS, 12), 1)

    def of_row(r):
        group, plane = (r // 24, r % 24)
        slot, lev = (group // 2, group % 2)
        comp, level = (plane // 11, plane % 11)
        layer = level - lev
        good = (plane < 22) & (layer >= 0) & (layer < 10)
        return comp * 6 + lev * 3 + slot, layer, good

    pick = jnp.where(of_row(row)[0] == col, 1.0, 0.0)
    r = lax.broadcasted_iota(jnp.int32, (GROUPS, 3 * HALF), 0)
    k = lax.broadcasted_iota(jnp.int32, (GROUPS, 3 * HALF), 1)
    _, layer, good = of_row(r)
    part = (k % HALF) // 24
    plane = (k % HALF) % 24
    lev_in = plane % 11 - layer
    good = good & (part < 3) & (plane < 22)
    q = lax.broadcasted_iota(jnp.int32, (12, 3 * HALF), 0)
    kq = lax.broadcasted_iota(jnp.int32, (12, 3 * HALF), 1)
    comp_in = ((kq % HALF) % 24) // 11
    block = kq // HALF
    for tri in range(2):
        first, second, third = ((0, 2, 1), (2, 0, 1))[tri]
        place = jnp.where(block == 0, first, jnp.where(block == 1, second, third))
        rows = jnp.dot(
            pick, stiff[tri], precision=lax.Precision.HIGHEST, preferred_element_type=jnp.float32
        )
        total = jnp.zeros((GROUPS, 3 * HALF), jnp.float32)
        for lev in range(2):
            sel = jnp.where(comp_in * 6 + lev * 3 + place == q, 1.0, 0.0)
            spread = jnp.dot(
                rows, sel, precision=lax.Precision.HIGHEST, preferred_element_type=jnp.float32
            )
            total = jnp.where(good & (lev_in == lev), spread, total)
        high = total.astype(jnp.bfloat16).astype(jnp.float32)
        weights[tri] = jnp.where(part == 2, total - high, high).astype(jnp.bfloat16)


def split_rows(x):
    high = x.astype(jnp.bfloat16).astype(jnp.float32)
    pad = jnp.zeros((HALF - 72, x.shape[1]), jnp.float32)
    return jnp.concatenate([high, x - high, high, pad], axis=0).astype(jnp.bfloat16)


def put_operand(operand, i, x):
    start = pl.multiple_of(i * BLOCK, BLOCK)
    operand[pl.ds(start, HALF), :] = split_rows(x)
    operand[pl.ds(start + HALF, HALF), :] = split_rows(pltpu.roll(x, LANES - 1, 1))


def main_kernel(
    own, first_rows, second_rows, first_cols, second_cols, stiff, weights,
    powers, gram,
    full, scale, diag, field, operand, carry,
):
    lane = lax.broadcasted_iota(jnp.int32, (48, 128), 1)
    odd_row = odd_along("rx")
    odd_col = odd_along("ry")
    from_left = jnp.where(odd_col, first_cols[...], second_cols[...])
    from_right = jnp.where(odd_col, second_cols[...], first_cols[...])
    theta = shift_of(stiff)
    plane = lax.broadcasted_iota(jnp.int32, (24, LANES), 0)
    bottom = (plane == 0) | (plane == 11)
    for i in range(NROW):
        row = full.at[i]
        if i < DEPTH:
            row[:, 0:512] = jnp.where(odd_row, first_rows[i], second_rows[i])
        elif i >= 8 + DEPTH:
            j = i - 8 - DEPTH
            row[:, 0:512] = jnp.where(odd_row, second_rows[j], first_rows[j])
        else:
            row[:, 0:512] = own[i - DEPTH]
        on_right = pltpu.roll(from_right, 128 - 8 * i, 1) if i else from_right
        on_left = pltpu.roll(from_left, (128 - DEPTH - 8 * i) % 128, 1)
        row[:, 512:640] = jnp.where(
            lane < DEPTH, on_right, jnp.where(lane >= 128 - DEPTH, on_left, 0.0)
        )
        real = row[22:23, :]
        x = jnp.where(plane < 22, row[0:24, :], 0.0)
        field[0, i] = x
        put_operand(operand.at[0], i, x)
        diag[i] = real * (1.0 - theta) + jnp.where(bottom, row[23:24, :], 0.0)
        if i < NROW - 1:
            for tri in range(2):
                coef = row[24 + 10 * tri : 34 + 10 * tri, :]
                for lev in range(2):
                    base = 48 * tri + 24 * lev
                    out = scale.at[i]
                    out[base : base + 24, :] = jnp.zeros((24, LANES), jnp.float32)
                    out[base + lev : base + lev + 10, :] = coef
                    out[base + 11 + lev : base + 21 + lev, :] = coef

    for step in range(1, DEPTH + 1):
        source = operand.at[(step - 1) % 2]
        target = operand.at[step % 2]
        carry[...] = jnp.zeros_like(carry)

        def cell_row(i, _, step=step, source=source, target=target):
            start = pl.multiple_of(i * BLOCK, BLOCK)
            mixed = [
                jnp.dot(
                    weights[tri],
                    source[pl.ds(start + HALF * tri, 3 * HALF), :],
                    preferred_element_type=jnp.float32,
                )
                for tri in range(2)
            ]
            grown = []
            for tri in range(2):
                upper = scale[i, 48 * tri : 48 * tri + 24, :]
                lower = scale[i, 48 * tri + 24 : 48 * tri + 48, :]
                for slot in range(3):
                    at = 48 * slot
                    grown.append(
                        upper * mixed[tri][at : at + 24] + lower * mixed[tri][at + 24 : at + 48]
                    )
            near = grown[0] + carry[0]
            far = grown[2] + grown[5] + carry[1]
            carry[0] = grown[1] + grown[3]
            carry[1] = grown[4]
            total = near + pltpu.roll(far, 1, 1)
            x = full[i, 22:23, :] * total + diag[i] * field[step - 1, i]
            field[step, i] = x
            if step < DEPTH:
                put_operand(target, i, x)
            return 0

        lax.fori_loop(step - 1, NROW - step, cell_row, 0, unroll=True)

    pairs = [(a, b) for a in range(4) for b in range(a, 4)]

    def add_row(r, sums):
        vectors = [field[a, r + DEPTH, :, 0:512] for a in range(4)]
        result = []
        for total, (a, b) in zip(sums, pairs):
            product = vectors[a] * vectors[b]
            for s in range(3):
                for l in range(4):
                    total = total + product[8 * s : 8 * s + 8, 128 * l : 128 * l + 128]
            result.append(total)
        for a in range(1, 4):
            powers[a - 1, r] = vectors[a]
        return tuple(result)

    sums = lax.fori_loop(
        0, 8, add_row, tuple(jnp.zeros((8, 128), jnp.float32) for _ in pairs)
    )
    place = lax.broadcasted_iota(jnp.int32, (8, 128), 1)
    line = jnp.zeros((8, 128), jnp.float32)
    for n, total in enumerate(sums):
        line = jnp.where(place == n, jnp.sum(total), line)
    devices = gram.shape[0]
    gram[...] = jnp.broadcast_to(line[0:1], (devices, 128))


def combine_kernel(own, powers, grams, stiff, update, last):
    theta = shift_of(stiff)
    entry = jnp.sum(grams[...], axis=0, keepdims=True)
    place = lax.broadcasted_iota(jnp.int32, (1, 128), 1)
    pairs = [(a, b) for a in range(4) for b in range(a, 4)]
    g = {}
    for n, pair in enumerate(pairs):
        g[pair] = jnp.sum(jnp.where(place == n, entry, 0.0), axis=1, keepdims=True)
    upper = [[None] * 4 for _ in range(4)]
    for a in range(4):
        for b in range(a, 4):
            value = g[a, b]
            for c in range(a):
                value = value - upper[c][a] * upper[c][b]
            if a == b:
                upper[a][a] = jnp.sqrt(value)
            else:
                upper[a][b] = value / upper[a][a]
    zero = jnp.zeros((1, 1), jnp.float32)
    table = [
        [
            (upper[a][b + 1] if a <= b + 1 else zero) + (theta * upper[a][b] if a <= b else zero)
            for b in range(3)
        ]
        for a in range(4)
    ]
    target = [upper[0][0], zero, zero, zero]
    for col in range(3):
        first, second = (table[col][col], table[col + 1][col])
        radius = jnp.sqrt(first * first + second * second)
        cosine, sine = (first / radius, second / radius)
        for c in range(col, 3):
            one, two = (table[col][c], table[col + 1][c])
            table[col][c] = cosine * one + sine * two
            table[col + 1][c] = cosine * two - sine * one
        one, two = (target[col], target[col + 1])
        target[col] = cosine * one + sine * two
        target[col + 1] = cosine * two - sine * one
    z = [None] * 3
    for col in (2, 1, 0):
        value = target[col]
        for c in range(col + 1, 3):
            value = value - table[col][c] * z[c]
        z[col] = value / table[col][col]
    w = [None] * 4
    w[3] = 1.0 / upper[3][3]
    for a in (2, 1, 0):
        value = zero
        for c in range(a + 1, 4):
            value = value - upper[a][c] * w[c]
        w[a] = value / upper[a][a]
    for r in range(8):
        one = own[r, 0:22, :]
        rest = [powers[a, r, 0:22, :] for a in range(3)]
        update[:, r, :] = z[0] * one + z[1] * rest[0] + z[2] * rest[1]
        last[:, r, :] = w[0] * one + w[1] * rest[0] + w[2] * rest[1] + w[3] * rest[2]


def call(kernel, outs, scratch=(), flops=0, bytes_accessed=0, limit=8):
    single = not isinstance(outs, (list, tuple))
    return pl.pallas_call(
        kernel,
        out_shape=outs if single else tuple(outs),
        scratch_shapes=list(scratch),
        compiler_params=pltpu.CompilerParams(vmem_limit_bytes=limit * 1024 * 1024),
        cost_estimate=pl.CostEstimate(
            flops=flops, bytes_accessed=bytes_accessed, transcendentals=0
        ),
    )


def f32(*shape):
    return jax.ShapeDtypeStruct(shape, jnp.float32)


def swapped(shard, axis, start):
    pairs = []
    for i in range(start, lax.axis_size(axis) - 1, 2):
        pairs += [(i, i + 1), (i + 1, i)]
    return lax.ppermute(shard, axis, pairs)


def body(rhs, viscosity, cell_mask, friction, stiffness):
    devices = lax.axis_size("rx") * lax.axis_size("ry")
    local = (rhs.reshape(22, 8, 512), viscosity, cell_mask, friction)
    first, second = call(
        rows_kernel, (f32(DEPTH, 48, 512),) * 2, [pltpu.VMEM((2, 48, 512), jnp.float32)], bytes_accessed=10**6
    )(*local)
    first_rows = swapped(first, "rx", 0)
    second_rows = swapped(second, "rx", 1)
    own, packs, weights = call(
        own_kernel,
        (f32(8, 48, 512), f32(2, 48, 128), jax.ShapeDtypeStruct((2, GROUPS, 3 * HALF), jnp.bfloat16)),
        flops=10**7,
        bytes_accessed=10**6,
    )(*local, stiffness)
    first, second = call(cols_kernel, (f32(48, 128),) * 2, bytes_accessed=10**6)(packs, first_rows, second_rows)
    first_cols = swapped(first, "ry", 0)
    second_cols = swapped(second, "ry", 1)
    powers, gram = call(
        main_kernel,
        (f32(3, 8, 24, 512), f32(devices, 128)),
        [
            pltpu.VMEM((NROW, 48, LANES), jnp.float32),
            pltpu.VMEM((NROW - 1, 96, LANES), jnp.float32),
            pltpu.VMEM((NROW, 24, LANES), jnp.float32),
            pltpu.VMEM((4, NROW, 24, LANES), jnp.float32),
            pltpu.VMEM((2, NROW * BLOCK, LANES), jnp.bfloat16),
            pltpu.VMEM((2, 24, LANES), jnp.float32),
        ],
        flops=3 * 10**9,
        bytes_accessed=3 * 10**6,
        limit=28,
    )(own, first_rows, second_rows, first_cols, second_cols, stiffness, weights)
    grams = lax.all_to_all(gram.reshape(devices, 1, 128), ("rx", "ry"), 0, 0)
    update, last = call(combine_kernel, (f32(22, 8, 512),) * 2, bytes_accessed=3 * 10**6)(
        own, powers, grams.reshape(devices, 128), stiffness
    )
    return update.reshape(2, 11, 8, 512), last.reshape(2, 11, 8, 512)


def solution(mesh):
    in_specs = (
        P(None, None, "rx", "ry"),
        P(None, None, "rx", "ry"),
        P("rx", "ry"),
        P("rx", "ry"),
        P(),
    )
    out_specs = (P(None, None, "rx", "ry"), P(None, None, "rx", "ry"))
    return jax.shard_map(body, mesh=mesh, in_specs=in_specs, out_specs=out_specs, check_vma=False)
```

```python
import jax
import jax.numpy as jnp
from jax import lax
from jax.experimental import pallas as pl
from jax.experimental.pallas import tpu as pltpu
from jax.sharding import PartitionSpec as P


DEPTH = 3
NROW = 8 + 2 * DEPTH
LANES = 512
PITCH = 18
EDGE = 256
PAIRS = [(a, b) for a in range(4) for b in range(a, 4)]
HALF = 80
BLOCK = 2 * HALF
GROUPS = 144


def shift_of(stiff):
    rows = lax.broadcasted_iota(jnp.int32, (12, 12), 0)
    cols = lax.broadcasted_iota(jnp.int32, (12, 12), 1)
    trace = jnp.sum(jnp.where(rows == cols, stiff[0] + stiff[1], 0.0))
    return 1.0 + trace * (1.2 * 10.0 / 22.0)


def own_row(out, rhs, visc, mask, fric, row):
    ice = mask[row : row + 1, :].astype(jnp.float32)
    out[0:22, 0:512] = rhs[:, row, :]
    out[22:23, 0:512] = jnp.ones_like(ice)
    out[23:24, 0:512] = fric[row : row + 1, :]
    out[24:34, 0:512] = visc[:, 0, row, :] * ice
    out[34:44, 0:512] = visc[:, 1, row, :] * ice
    out[44:48, 0:512] = jnp.zeros((4, 512), jnp.float32)


def odd_along(axis):
    return lax.rem(lax.axis_index(axis), 2) == 1


def rows_kernel(rhs, visc, mask, fric, first, second, rhs_out, visc_out, mask_out, fric_out, work, sems):
    copies = [
        pltpu.make_async_copy(src, dst, sems.at[n])
        for n, (src, dst) in enumerate(
            ((rhs, rhs_out), (visc, visc_out), (mask, mask_out), (fric, fric_out))
        )
    ]
    for copy in copies:
        copy.start()
    for copy in copies:
        copy.wait()
    odd = odd_along("rx")
    for j in range(DEPTH):
        own_row(work.at[0], rhs_out, visc_out, mask_out, fric_out, 8 - DEPTH + j)
        own_row(work.at[1], rhs_out, visc_out, mask_out, fric_out, j)
        up, down = (work[0], work[1])
        first[j] = jnp.where(odd, down, up)
        second[j] = jnp.where(odd, up, down)


def pack_row(row, i, lane, packed):
    ends = jnp.concatenate([row[:, 0:128], row[:, 384:512]], axis=1)
    at = lane - PITCH * i
    packed = jnp.where((at >= 0) & (at < 9), pltpu.roll(ends, (PITCH * i + 3) % EDGE, 1), packed)
    return jnp.where((at >= 9) & (at < 18), pltpu.roll(ends, (PITCH * i + 15) % EDGE, 1), packed)


def own_kernel(rhs, visc, mask, fric, stiff, own, packs, weights):
    weights_kernel(stiff, weights)
    lane = lax.broadcasted_iota(jnp.int32, (48, EDGE), 1)
    packed = jnp.zeros((48, EDGE), jnp.float32)
    for r in range(8):
        own_row(own.at[r], rhs, visc, mask, fric, r)
        packed = pack_row(own.at[r], r + DEPTH, lane, packed)
    packs[...] = packed


def cols_kernel(packs, first_rows, second_rows, out):
    odd_row = odd_along("rx")
    lane = lax.broadcasted_iota(jnp.int32, (48, EDGE), 1)
    packed = packs[...]
    for j in range(DEPTH):
        one, two = (first_rows[j], second_rows[j])
        packed = pack_row(jnp.where(odd_row, one, two), j, lane, packed)
        packed = pack_row(jnp.where(odd_row, two, one), j + 8 + DEPTH, lane, packed)
    out[...] = packed


def weights_kernel(stiff, weights):
    row = lax.broadcasted_iota(jnp.int32, (GROUPS, 12), 0)
    col = lax.broadcasted_iota(jnp.int32, (GROUPS, 12), 1)

    def of_row(r):
        group, plane = (r // 24, r % 24)
        slot, lev = (group // 2, group % 2)
        comp, level = (plane // 11, plane % 11)
        layer = level - lev
        good = (plane < 22) & (layer >= 0) & (layer < 10)
        return comp * 6 + lev * 3 + slot, layer, good

    pick = jnp.where(of_row(row)[0] == col, 1.0, 0.0)
    r = lax.broadcasted_iota(jnp.int32, (GROUPS, 3 * HALF), 0)
    k = lax.broadcasted_iota(jnp.int32, (GROUPS, 3 * HALF), 1)
    _, layer, good = of_row(r)
    part = (k % HALF) // 24
    plane = (k % HALF) % 24
    lev_in = plane % 11 - layer
    good = good & (part < 3) & (plane < 22)
    q = lax.broadcasted_iota(jnp.int32, (12, 3 * HALF), 0)
    kq = lax.broadcasted_iota(jnp.int32, (12, 3 * HALF), 1)
    comp_in = ((kq % HALF) % 24) // 11
    block = kq // HALF
    for tri in range(2):
        first, second, third = ((0, 2, 1), (2, 0, 1))[tri]
        place = jnp.where(block == 0, first, jnp.where(block == 1, second, third))
        rows = jnp.dot(
            pick, stiff[tri], precision=lax.Precision.HIGHEST, preferred_element_type=jnp.float32
        )
        total = jnp.zeros((GROUPS, 3 * HALF), jnp.float32)
        for lev in range(2):
            sel = jnp.where(comp_in * 6 + lev * 3 + place == q, 1.0, 0.0)
            spread = jnp.dot(
                rows, sel, precision=lax.Precision.HIGHEST, preferred_element_type=jnp.float32
            )
            total = jnp.where(good & (lev_in == lev), spread, total)
        high = total.astype(jnp.bfloat16).astype(jnp.float32)
        weights[tri] = jnp.where(part == 2, total - high, high).astype(jnp.bfloat16)


def split_rows(x):
    high = x.astype(jnp.bfloat16).astype(jnp.float32)
    pad = jnp.zeros((HALF - 72, x.shape[1]), jnp.float32)
    return jnp.concatenate([high, x - high, high, pad], axis=0).astype(jnp.bfloat16)


def put_operand(operand, i, x):
    operand[i * BLOCK : i * BLOCK + HALF, :] = split_rows(x)
    operand[i * BLOCK + HALF : (i + 1) * BLOCK, :] = split_rows(pltpu.roll(x, LANES - 1, 1))


def put_scale(out, coefs):
    zeros = jnp.zeros((24, out.shape[1]), jnp.float32)
    for tri in range(2):
        for lev in range(2):
            base = 48 * tri + 24 * lev
            out[base : base + 24, :] = zeros
            out[base + lev : base + lev + 10, :] = coefs[tri]
            out[base + 11 + lev : base + 21 + lev, :] = coefs[tri]


def grown_of(scale, mixed):
    parts = []
    for tri in range(2):
        upper = scale[48 * tri : 48 * tri + 24, :]
        lower = scale[48 * tri + 24 : 48 * tri + 48, :]
        for slot in range(3):
            at = 48 * slot
            parts.append(upper * mixed[tri][at : at + 24] + lower * mixed[tri][at + 24 : at + 48])
    return parts[0], parts[1] + parts[3], parts[2] + parts[5], parts[4]


def inner_products(vectors, sums, lanes):
    result = []
    for total, (a, b) in zip(sums, PAIRS):
        product = vectors[a] * vectors[b]
        for s in range(0, 24, 8):
            for l in range(0, lanes, 128):
                total = total + product[s : s + 8, l : l + 128]
        result.append(total)
    return tuple(result)


def line_of(sums):
    place = lax.broadcasted_iota(jnp.int32, (8, 128), 1)
    line = jnp.zeros((8, 128), jnp.float32)
    for n, total in enumerate(sums):
        line = jnp.where(place == n, jnp.sum(total), line)
    return line


def no_sums():
    return tuple(jnp.zeros((8, 128), jnp.float32) for _ in PAIRS)


def main_kernel(
    own, first_rows, second_rows, stiff, weights, powers, line, scale, diag, field, operand, carry
):
    odd_row = odd_along("rx")
    theta = shift_of(stiff)
    plane = lax.broadcasted_iota(jnp.int32, (24, LANES), 0)
    bottom = (plane == 0) | (plane == 11)
    real = {}
    for i in range(NROW):
        if i < DEPTH:
            row = jnp.where(odd_row, first_rows[i], second_rows[i])
        elif i >= 8 + DEPTH:
            j = i - 8 - DEPTH
            row = jnp.where(odd_row, second_rows[j], first_rows[j])
            real[i] = row[22:23, :]
        else:
            row = own[i - DEPTH]
        x = jnp.where(plane < 22, row[0:24, :], 0.0)
        field[0, i] = x
        put_operand(operand.at[0], i, x)
        diag[i] = row[22:23, :] * (1.0 - theta) + jnp.where(bottom, row[23:24, :], 0.0)
        if i < NROW - 1:
            put_scale(scale.at[i], (row[24:34, :], row[34:44, :]))

    for step in range(1, DEPTH + 1):
        source = operand.at[(step - 1) % 2]
        target = operand.at[step % 2]
        carry[...] = jnp.zeros_like(carry)
        for i in range(step - 1, NROW - step):
            start = i * BLOCK
            mixed = [
                jnp.dot(
                    weights[tri],
                    source[start + HALF * tri : start + HALF * tri + 3 * HALF, :],
                    preferred_element_type=jnp.float32,
                )
                for tri in range(2)
            ]
            a, b, c, d = grown_of(scale[i], mixed)
            total = a + carry[0] + pltpu.roll(c + carry[1], 1, 1)
            carry[0] = b
            carry[1] = d
            if i in real:
                total = total * real[i]
            x = total + diag[i] * field[step - 1, i]
            field[step, i] = x
            if DEPTH <= i < DEPTH + 8:
                powers[step - 1, i - DEPTH] = x
            if step < DEPTH:
                put_operand(target, i, x)

    lane = lax.broadcasted_iota(jnp.int32, (24, LANES), 1)
    inside = (lane >= DEPTH) & (lane < LANES - DEPTH)
    sums = no_sums()
    for r in range(8):
        vectors = [jnp.where(inside, field[a, r + DEPTH], 0.0) for a in range(4)]
        sums = inner_products(vectors, sums, LANES)
    line[...] = line_of(sums)


def edge_kernel(packs, first_cols, second_cols, stiff, weights, line, edges, gram, scale):
    odd_col = odd_along("ry")
    theta = shift_of(stiff)
    at = lax.rem(lax.broadcasted_iota(jnp.int32, (48, EDGE), 1), PITCH)
    from_left = jnp.where(odd_col, first_cols[...], second_cols[...])
    from_right = jnp.where(odd_col, second_cols[...], first_cols[...])
    full = jnp.where(at < 3, from_left, jnp.where(at >= 15, from_right, packs[...]))
    plane = lax.broadcasted_iota(jnp.int32, (24, EDGE), 0)
    bottom = (plane == 0) | (plane == 11)
    put_scale(scale, (full[24:34], full[34:44]))
    real = full[22:23]
    diag = real * (1.0 - theta) + jnp.where(bottom, full[23:24], 0.0)
    x = jnp.where(plane < 22, full[0:24], 0.0)
    vectors = [x]
    for _ in range(DEPTH):
        corners = [
            split_rows(pltpu.roll(x, (EDGE - by) % EDGE, 1) if by else x)
            for by in (0, 1, PITCH, PITCH + 1)
        ]
        mixed = [
            jnp.dot(
                weights[tri],
                jnp.concatenate(corners[tri : tri + 3], axis=0),
                preferred_element_type=jnp.float32,
            )
            for tri in range(2)
        ]
        a, b, c, d = grown_of(scale[...], mixed)
        total = a + pltpu.roll(b, PITCH, 1) + pltpu.roll(c + pltpu.roll(d, PITCH, 1), 1, 1)
        x = real * total + diag * x
        vectors.append(x)
    for a in range(4):
        edges[a] = vectors[a]
    lane = lax.broadcasted_iota(jnp.int32, (24, EDGE), 1)
    at = lax.rem(lane, PITCH)
    mine = (lane >= PITCH * DEPTH) & (lane < PITCH * (DEPTH + 8))
    mine = mine & (((at >= 3) & (at < 6)) | ((at >= 12) & (at < 15)))
    sums = inner_products([jnp.where(mine, v, 0.0) for v in vectors], no_sums(), EDGE)
    total = line[...] + line_of(sums)
    gram[...] = jnp.broadcast_to(total[0:1], gram.shape)


def combine_kernel(own, powers, edges, grams, stiff, update, last):
    theta = shift_of(stiff)
    entry = jnp.sum(grams[...], axis=0, keepdims=True)
    place = lax.broadcasted_iota(jnp.int32, (1, 128), 1)
    g = {}
    for n, pair in enumerate(PAIRS):
        g[pair] = jnp.sum(jnp.where(place == n, entry, 0.0), axis=1, keepdims=True)
    upper = [[None] * 4 for _ in range(4)]
    for a in range(4):
        for b in range(a, 4):
            value = g[a, b]
            for c in range(a):
                value = value - upper[c][a] * upper[c][b]
            if a == b:
                upper[a][a] = jnp.sqrt(value)
            else:
                upper[a][b] = value / upper[a][a]
    zero = jnp.zeros((1, 1), jnp.float32)
    table = [
        [
            (upper[a][b + 1] if a <= b + 1 else zero) + (theta * upper[a][b] if a <= b else zero)
            for b in range(3)
        ]
        for a in range(4)
    ]
    target = [upper[0][0], zero, zero, zero]
    for col in range(3):
        first, second = (table[col][col], table[col + 1][col])
        radius = jnp.sqrt(first * first + second * second)
        cosine, sine = (first / radius, second / radius)
        for c in range(col, 3):
            one, two = (table[col][c], table[col + 1][c])
            table[col][c] = cosine * one + sine * two
            table[col + 1][c] = cosine * two - sine * one
        one, two = (target[col], target[col + 1])
        target[col] = cosine * one + sine * two
        target[col + 1] = cosine * two - sine * one
    z = [None] * 3
    for col in (2, 1, 0):
        value = target[col]
        for c in range(col + 1, 3):
            value = value - table[col][c] * z[c]
        z[col] = value / table[col][col]
    w = [None] * 4
    w[3] = 1.0 / upper[3][3]
    for a in (2, 1, 0):
        value = zero
        for c in range(a + 1, 4):
            value = value - upper[a][c] * w[c]
        w[a] = value / upper[a][a]
    lane = lax.broadcasted_iota(jnp.int32, (22, 128), 1)
    for out, factors in ((update, z), (last, w)):
        ends = factors[0] * edges[0]
        for a in range(1, len(factors)):
            ends = ends + factors[a] * edges[a]
        for r in range(8):
            row = factors[0] * own[r, 0:22, :]
            for a in range(1, len(factors)):
                row = row + factors[a] * powers[a - 1, r, 0:22, :]
            at = PITCH * (r + DEPTH)
            left = pltpu.roll(ends, (EDGE - at - 3) % EDGE, 1)[0:22, 0:128]
            right = pltpu.roll(ends, (253 - at - 12) % EDGE, 1)[0:22, 128:256]
            out[:, r, 0:128] = jnp.where(lane < DEPTH, left, row[:, 0:128])
            out[:, r, 128:384] = row[:, 128:384]
            out[:, r, 384:512] = jnp.where(lane >= 128 - DEPTH, right, row[:, 384:512])


def call(kernel, outs, scratch=(), flops=0, bytes_accessed=0, limit=8, in_hbm=0):
    single = not isinstance(outs, (list, tuple))
    extra = {"in_specs": [pl.BlockSpec(memory_space=pltpu.HBM)] * in_hbm} if in_hbm else {}
    return pl.pallas_call(
        kernel,
        out_shape=outs if single else tuple(outs),
        scratch_shapes=list(scratch),
        **extra,
        compiler_params=pltpu.CompilerParams(vmem_limit_bytes=limit * 1024 * 1024),
        cost_estimate=pl.CostEstimate(
            flops=flops, bytes_accessed=bytes_accessed, transcendentals=0
        ),
    )


def f32(*shape):
    return jax.ShapeDtypeStruct(shape, jnp.float32)


def swapped(shard, axis, start):
    pairs = []
    for i in range(start, lax.axis_size(axis) - 1, 2):
        pairs += [(i, i + 1), (i + 1, i)]
    return lax.ppermute(shard, axis, pairs)


def body(rhs, viscosity, cell_mask, friction, stiffness):
    devices = lax.axis_size("rx") * lax.axis_size("ry")
    natural = [
        pltpu.with_memory_space_constraint(x, pltpu.HBM)
        for x in (rhs.reshape(22, 8, 512), viscosity, cell_mask, friction)
    ]
    first, second, *local = call(
        rows_kernel,
        (f32(DEPTH, 48, 512), f32(DEPTH, 48, 512), f32(22, 8, 512), f32(10, 2, 8, 512),
         jax.ShapeDtypeStruct((8, 512), jnp.int32), f32(8, 512)),
        [pltpu.VMEM((2, 48, 512), jnp.float32), pltpu.SemaphoreType.DMA((4,))],
        bytes_accessed=10**6,
        in_hbm=4,
    )(*natural)
    first_rows = swapped(first, "rx", 0)
    second_rows = swapped(second, "rx", 1)
    own, packs, weights = call(
        own_kernel,
        (f32(8, 48, 512), f32(48, EDGE), jax.ShapeDtypeStruct((2, GROUPS, 3 * HALF), jnp.bfloat16)),
        flops=10**7,
        bytes_accessed=10**6,
    )(*local, stiffness)
    packs = call(cols_kernel, f32(48, EDGE), bytes_accessed=10**6)(packs, first_rows, second_rows)
    first_cols = swapped(packs, "ry", 0)
    second_cols = swapped(packs, "ry", 1)
    powers, line = call(
        main_kernel,
        (f32(3, 8, 24, LANES), f32(8, 128)),
        [
            pltpu.VMEM((NROW - 1, 96, LANES), jnp.float32),
            pltpu.VMEM((NROW, 24, LANES), jnp.float32),
            pltpu.VMEM((4, NROW, 24, LANES), jnp.float32),
            pltpu.VMEM((2, NROW * BLOCK, LANES), jnp.bfloat16),
            pltpu.VMEM((2, 24, LANES), jnp.float32),
        ],
        flops=3 * 10**9,
        bytes_accessed=3 * 10**6,
        limit=28,
    )(own, first_rows, second_rows, stiffness, weights)
    edges, gram = call(
        edge_kernel,
        (f32(4, 24, EDGE), f32(devices, 128)),
        [pltpu.VMEM((96, EDGE), jnp.float32)],
        flops=10**8,
        bytes_accessed=10**6,
    )(packs, first_cols, second_cols, stiffness, weights, line)
    grams = lax.all_to_all(gram.reshape(devices, 1, 128), ("rx", "ry"), 0, 0)
    update, last = call(combine_kernel, (f32(22, 8, 512),) * 2, bytes_accessed=3 * 10**6)(
        own, powers, edges, grams.reshape(devices, 128), stiffness
    )
    return update.reshape(2, 11, 8, 512), last.reshape(2, 11, 8, 512)


def solution(mesh):
    in_specs = (
        P(None, None, "rx", "ry"),
        P(None, None, "rx", "ry"),
        P("rx", "ry"),
        P("rx", "ry"),
        P(),
    )
    out_specs = (P(None, None, "rx", "ry"), P(None, None, "rx", "ry"))
    return jax.shard_map(body, mesh=mesh, in_specs=in_specs, out_specs=out_specs, check_vma=False)
```

```python
import jax
import jax.numpy as jnp
from jax import lax
from jax.experimental import pallas as pl
from jax.experimental.pallas import tpu as pltpu
from jax.sharding import PartitionSpec as P


DEPTH = 3
NROW = 8 + 2 * DEPTH
LANES = 512
PITCH = 18
EDGE = 256
PAIRS = [(a, b) for a in range(4) for b in range(a, 4)]
HALF = 80
BLOCK = 2 * HALF
GROUPS = 144


def shift_of(stiff):
    rows = lax.broadcasted_iota(jnp.int32, (12, 12), 0)
    cols = lax.broadcasted_iota(jnp.int32, (12, 12), 1)
    trace = jnp.sum(jnp.where(rows == cols, stiff[0] + stiff[1], 0.0))
    return 1.0 + trace * (1.2 * 10.0 / 22.0)


def own_row(out, rhs, visc, mask, fric, row):
    ice = mask[row : row + 1, :].astype(jnp.float32)
    out[0:22, 0:512] = rhs[:, row, :]
    out[22:23, 0:512] = jnp.ones_like(ice)
    out[23:24, 0:512] = fric[row : row + 1, :]
    out[24:34, 0:512] = visc[:, 0, row, :] * ice
    out[34:44, 0:512] = visc[:, 1, row, :] * ice
    out[44:48, 0:512] = jnp.zeros((4, 512), jnp.float32)


def odd_along(axis):
    return lax.rem(lax.axis_index(axis), 2) == 1


def rows_kernel(rhs, visc, mask, fric, first, second, rhs_out, visc_out, mask_out, fric_out, work, sems):
    copies = [
        pltpu.make_async_copy(src, dst, sems.at[n])
        for n, (src, dst) in enumerate(
            ((rhs, rhs_out), (visc, visc_out), (mask, mask_out), (fric, fric_out))
        )
    ]
    for copy in copies:
        copy.start()
    for copy in copies:
        copy.wait()
    odd = odd_along("rx")
    for j in range(DEPTH):
        own_row(work.at[0], rhs_out, visc_out, mask_out, fric_out, 8 - DEPTH + j)
        own_row(work.at[1], rhs_out, visc_out, mask_out, fric_out, j)
        up, down = (work[0], work[1])
        first[j] = jnp.where(odd, down, up)
        second[j] = jnp.where(odd, up, down)


def pack_row(row, i, lane, packed):
    ends = jnp.concatenate([row[:, 0:128], row[:, 384:512]], axis=1)
    at = lane - PITCH * i
    packed = jnp.where((at >= 0) & (at < 9), pltpu.roll(ends, (PITCH * i + 3) % EDGE, 1), packed)
    return jnp.where((at >= 9) & (at < 18), pltpu.roll(ends, (PITCH * i + 15) % EDGE, 1), packed)


def cols_kernel(packs, first_rows, second_rows, out):
    odd_row = odd_along("rx")
    lane = lax.broadcasted_iota(jnp.int32, (48, EDGE), 1)
    packed = packs[...]
    for j in range(DEPTH):
        one, two = (first_rows[j], second_rows[j])
        packed = pack_row(jnp.where(odd_row, one, two), j, lane, packed)
        packed = pack_row(jnp.where(odd_row, two, one), j + 8 + DEPTH, lane, packed)
    out[...] = packed


def weights_kernel(stiff, weights):
    row = lax.broadcasted_iota(jnp.int32, (GROUPS, 12), 0)
    col = lax.broadcasted_iota(jnp.int32, (GROUPS, 12), 1)

    def of_row(r):
        group, plane = (r // 24, r % 24)
        slot, lev = (group // 2, group % 2)
        comp, level = (plane // 11, plane % 11)
        layer = level - lev
        good = (plane < 22) & (layer >= 0) & (layer < 10)
        return comp * 6 + lev * 3 + slot, layer, good

    pick = jnp.where(of_row(row)[0] == col, 1.0, 0.0)
    r = lax.broadcasted_iota(jnp.int32, (GROUPS, 3 * HALF), 0)
    k = lax.broadcasted_iota(jnp.int32, (GROUPS, 3 * HALF), 1)
    _, layer, good = of_row(r)
    part = (k % HALF) // 24
    plane = (k % HALF) % 24
    lev_in = plane % 11 - layer
    good = good & (part < 3) & (plane < 22)
    q = lax.broadcasted_iota(jnp.int32, (12, 3 * HALF), 0)
    kq = lax.broadcasted_iota(jnp.int32, (12, 3 * HALF), 1)
    comp_in = ((kq % HALF) % 24) // 11
    block = kq // HALF
    for tri in range(2):
        first, second, third = ((0, 2, 1), (2, 0, 1))[tri]
        place = jnp.where(block == 0, first, jnp.where(block == 1, second, third))
        rows = jnp.dot(
            pick, stiff[tri], precision=lax.Precision.HIGHEST, preferred_element_type=jnp.float32
        )
        total = jnp.zeros((GROUPS, 3 * HALF), jnp.float32)
        for lev in range(2):
            sel = jnp.where(comp_in * 6 + lev * 3 + place == q, 1.0, 0.0)
            spread = jnp.dot(
                rows, sel, precision=lax.Precision.HIGHEST, preferred_element_type=jnp.float32
            )
            total = jnp.where(good & (lev_in == lev), spread, total)
        high = total.astype(jnp.bfloat16).astype(jnp.float32)
        weights[tri] = jnp.where(part == 2, total - high, high).astype(jnp.bfloat16)


def split_rows(x):
    high = x.astype(jnp.bfloat16).astype(jnp.float32)
    pad = jnp.zeros((HALF - 72, x.shape[1]), jnp.float32)
    return jnp.concatenate([high, x - high, high, pad], axis=0).astype(jnp.bfloat16)


def put_operand(operand, i, x):
    operand[i * BLOCK : i * BLOCK + HALF, :] = split_rows(x)
    operand[i * BLOCK + HALF : (i + 1) * BLOCK, :] = split_rows(pltpu.roll(x, LANES - 1, 1))


def put_scale(out, coefs):
    zeros = jnp.zeros((24, out.shape[1]), jnp.float32)
    for tri in range(2):
        for lev in range(2):
            base = 48 * tri + 24 * lev
            out[base : base + 24, :] = zeros
            out[base + lev : base + lev + 10, :] = coefs[tri]
            out[base + 11 + lev : base + 21 + lev, :] = coefs[tri]


def grown_of(scale, mixed):
    parts = []
    for tri in range(2):
        upper = scale[48 * tri : 48 * tri + 24, :]
        lower = scale[48 * tri + 24 : 48 * tri + 48, :]
        for slot in range(3):
            at = 48 * slot
            parts.append(upper * mixed[tri][at : at + 24] + lower * mixed[tri][at + 24 : at + 48])
    return parts[0], parts[1] + parts[3], parts[2] + parts[5], parts[4]


def inner_products(vectors, sums, lanes):
    result = []
    for total, (a, b) in zip(sums, PAIRS):
        product = vectors[a] * vectors[b]
        for s in range(0, 24, 8):
            for l in range(0, lanes, 128):
                total = total + product[s : s + 8, l : l + 128]
        result.append(total)
    return tuple(result)


def line_of(sums):
    place = lax.broadcasted_iota(jnp.int32, (8, 128), 1)
    line = jnp.zeros((8, 128), jnp.float32)
    for n, total in enumerate(sums):
        line = jnp.where(place == n, jnp.sum(total), line)
    return line


def no_sums():
    return tuple(jnp.zeros((8, 128), jnp.float32) for _ in PAIRS)


def products(weights, source, i):
    start = i * BLOCK
    return [
        jnp.dot(
            weights[tri],
            source[start + HALF * tri : start + HALF * (tri + 3), :],
            preferred_element_type=jnp.float32,
        )
        for tri in range(2)
    ]


def bottom_planes(lanes):
    plane = lax.broadcasted_iota(jnp.int32, (24, lanes), 0)
    return (plane == 0) | (plane == 11)


def field_planes(row):
    plane = lax.broadcasted_iota(jnp.int32, (24, row.shape[1]), 0)
    return jnp.where(plane < 22, row[0:24, :], 0.0)


def diag_planes(row, theta):
    on_bottom = jnp.where(bottom_planes(row.shape[1]), row[23:24, :], 0.0)
    return row[22:23, :] * (1.0 - theta) + on_bottom


def is_inner(k, i):
    return DEPTH + k <= i <= DEPTH + 7 - k


def own_kernel(
    rhs, visc, mask, fric, stiff,
    own, packs, weights, scale, diag, powers, bounds, low_parts, high_parts,
    operand,
):
    weights_kernel(stiff, weights)
    theta = shift_of(stiff)
    lane = lax.broadcasted_iota(jnp.int32, (48, EDGE), 1)
    packed = jnp.zeros((48, EDGE), jnp.float32)
    for r in range(8):
        own_row(own.at[r], rhs, visc, mask, fric, r)
        row = own[r]
        packed = pack_row(row, r + DEPTH, lane, packed)
        put_operand(operand.at[0], r, field_planes(row))
        diag[r] = diag_planes(row, theta)
        put_scale(scale.at[r], (row[24:34, :], row[34:44, :]))
    packs[...] = packed
    for step in range(1, DEPTH + 1):
        source = operand.at[(step - 1) % 2]
        target = operand.at[step % 2]
        first, last = (step - 1, 8 - step)
        bounds[step - 1, 0] = source[first * BLOCK : (first + 1) * BLOCK, :]
        bounds[step - 1, 1] = source[last * BLOCK : (last + 1) * BLOCK, :]
        for r in range(first, last):
            a, b, c, d = grown_of(scale[r], products(weights, source, r))
            if r == first:
                low_parts[step - 1] = a + pltpu.roll(c, 1, 1)
            else:
                total = a + upper + pltpu.roll(c + across, 1, 1)
                before = powers[step - 2, r] if step > 1 else field_planes(own[r])
                x = total + diag[r] * before
                powers[step - 1, r] = x
                if step < DEPTH:
                    put_operand(target, r, x)
            upper, across = (b, d)
        high_parts[step - 1, 0] = upper
        high_parts[step - 1, 1] = across


def main_kernel(
    own, weights, own_scale, own_diag, inner, bounds, low_parts, high_parts, first_rows, second_rows, stiff,
    outer, line,
    scale, diag, field, operand,
):
    odd_row = odd_along("rx")
    theta = shift_of(stiff)
    real = {}
    for i in (0, 1, 2, 11, 12, 13):
        if i < DEPTH:
            row = jnp.where(odd_row, first_rows[i], second_rows[i])
        else:
            j = i - 8 - DEPTH
            row = jnp.where(odd_row, second_rows[j], first_rows[j])
            real[i] = row[22:23, :]
        x = field_planes(row)
        field[0, i] = x
        put_operand(operand.at[0], i, x)
        diag[i] = diag_planes(row, theta)
        if i < NROW - 1:
            put_scale(scale.at[i], (row[24:34, :], row[34:44, :]))

    def power(k, i):
        if k == 0 and is_inner(0, i):
            return field_planes(own[i - DEPTH])
        return inner[k - 1, i - DEPTH] if is_inner(k, i) else field[k, i]

    for step in range(1, DEPTH + 1):
        source = operand.at[(step - 1) % 2]
        target = operand.at[step % 2]
        for side, i in ((0, DEPTH + step - 1), (1, DEPTH + 8 - step)):
            source[i * BLOCK : (i + 1) * BLOCK, :] = bounds[step - 1, side]

        def grown(i, source=source):
            is_own = is_inner(0, i)
            return grown_of(own_scale[i - DEPTH] if is_own else scale[i], products(weights, source, i))

        def put(i, total, step=step, target=target):
            if i in real:
                total = total * real[i]
            x = total + (own_diag[i - DEPTH] if is_inner(0, i) else diag[i]) * power(step - 1, i)
            field[step, i] = x
            if is_inner(0, i):
                outer[step - 1, i - DEPTH] = x
            if step < DEPTH:
                put_operand(target, i, x)

        first = step - 1
        _, upper, _, across = grown(first)
        for i in range(first + 1, first + 3):
            a, b, c, d = grown(i)
            put(i, a + upper + pltpu.roll(c + across, 1, 1))
            upper, across = (b, d)
        put(first + 3, low_parts[step - 1] + upper + pltpu.roll(across, 1, 1))
        upper, across = (high_parts[step - 1, 0], high_parts[step - 1, 1])
        for i in range(11 - step, 14 - step):
            a, b, c, d = grown(i)
            put(i, a + upper + pltpu.roll(c + across, 1, 1))
            upper, across = (b, d)

    lane = lax.broadcasted_iota(jnp.int32, (24, LANES), 1)
    inside = (lane >= DEPTH) & (lane < LANES - DEPTH)
    sums = no_sums()
    for r in range(8):
        vectors = [jnp.where(inside, power(a, r + DEPTH), 0.0) for a in range(4)]
        sums = inner_products(vectors, sums, LANES)
    line[...] = line_of(sums)


def edge_kernel(packs, first_cols, second_cols, stiff, weights, line, edges, gram, scale):
    odd_col = odd_along("ry")
    theta = shift_of(stiff)
    at = lax.rem(lax.broadcasted_iota(jnp.int32, (48, EDGE), 1), PITCH)
    from_left = jnp.where(odd_col, first_cols[...], second_cols[...])
    from_right = jnp.where(odd_col, second_cols[...], first_cols[...])
    full = jnp.where(at < 3, from_left, jnp.where(at >= 15, from_right, packs[...]))
    put_scale(scale, (full[24:34], full[34:44]))
    real = full[22:23]
    diag = diag_planes(full, theta)
    x = field_planes(full)
    vectors = [x]
    for _ in range(DEPTH):
        corners = [
            split_rows(pltpu.roll(x, (EDGE - by) % EDGE, 1) if by else x)
            for by in (0, 1, PITCH, PITCH + 1)
        ]
        mixed = [
            jnp.dot(
                weights[tri],
                jnp.concatenate(corners[tri : tri + 3], axis=0),
                preferred_element_type=jnp.float32,
            )
            for tri in range(2)
        ]
        a, b, c, d = grown_of(scale[...], mixed)
        total = a + pltpu.roll(b, PITCH, 1) + pltpu.roll(c + pltpu.roll(d, PITCH, 1), 1, 1)
        x = real * total + diag * x
        vectors.append(x)
    for a in range(4):
        edges[a] = vectors[a]
    lane = lax.broadcasted_iota(jnp.int32, (24, EDGE), 1)
    at = lax.rem(lane, PITCH)
    mine = (lane >= PITCH * DEPTH) & (lane < PITCH * (DEPTH + 8))
    mine = mine & (((at >= 3) & (at < 6)) | ((at >= 12) & (at < 15)))
    sums = inner_products([jnp.where(mine, v, 0.0) for v in vectors], no_sums(), EDGE)
    total = line[...] + line_of(sums)
    gram[...] = jnp.broadcast_to(total[0:1], gram.shape)


def combine_kernel(own, inner, outer, edges, grams, stiff, update, last):
    theta = shift_of(stiff)
    entry = jnp.sum(grams[...], axis=0, keepdims=True)
    place = lax.broadcasted_iota(jnp.int32, (1, 128), 1)
    g = {}
    for n, pair in enumerate(PAIRS):
        g[pair] = jnp.sum(jnp.where(place == n, entry, 0.0), axis=1, keepdims=True)
    upper = [[None] * 4 for _ in range(4)]
    for a in range(4):
        for b in range(a, 4):
            value = g[a, b]
            for c in range(a):
                value = value - upper[c][a] * upper[c][b]
            if a == b:
                upper[a][a] = jnp.sqrt(value)
            else:
                upper[a][b] = value / upper[a][a]
    zero = jnp.zeros((1, 1), jnp.float32)
    table = [
        [
            (upper[a][b + 1] if a <= b + 1 else zero) + (theta * upper[a][b] if a <= b else zero)
            for b in range(3)
        ]
        for a in range(4)
    ]
    target = [upper[0][0], zero, zero, zero]
    for col in range(3):
        first, second = (table[col][col], table[col + 1][col])
        radius = jnp.sqrt(first * first + second * second)
        cosine, sine = (first / radius, second / radius)
        for c in range(col, 3):
            one, two = (table[col][c], table[col + 1][c])
            table[col][c] = cosine * one + sine * two
            table[col + 1][c] = cosine * two - sine * one
        one, two = (target[col], target[col + 1])
        target[col] = cosine * one + sine * two
        target[col + 1] = cosine * two - sine * one
    z = [None] * 3
    for col in (2, 1, 0):
        value = target[col]
        for c in range(col + 1, 3):
            value = value - table[col][c] * z[c]
        z[col] = value / table[col][col]
    w = [None] * 4
    w[3] = 1.0 / upper[3][3]
    for a in (2, 1, 0):
        value = zero
        for c in range(a + 1, 4):
            value = value - upper[a][c] * w[c]
        w[a] = value / upper[a][a]
    lane = lax.broadcasted_iota(jnp.int32, (22, 128), 1)
    for out, factors in ((update, z), (last, w)):
        ends = factors[0] * edges[0]
        for a in range(1, len(factors)):
            ends = ends + factors[a] * edges[a]
        for r in range(8):
            row = factors[0] * own[r, 0:22, :]
            for a in range(1, len(factors)):
                part = inner if is_inner(a, r + DEPTH) else outer
                row = row + factors[a] * part[a - 1, r, 0:22, :]
            at = PITCH * (r + DEPTH)
            left = pltpu.roll(ends, (EDGE - at - 3) % EDGE, 1)[0:22, 0:128]
            right = pltpu.roll(ends, (253 - at - 12) % EDGE, 1)[0:22, 128:256]
            out[:, r, 0:128] = jnp.where(lane < DEPTH, left, row[:, 0:128])
            out[:, r, 128:384] = row[:, 128:384]
            out[:, r, 384:512] = jnp.where(lane >= 128 - DEPTH, right, row[:, 384:512])


def call(kernel, outs, scratch=(), flops=0, bytes_accessed=0, limit=8, in_hbm=0):
    single = not isinstance(outs, (list, tuple))
    extra = {"in_specs": [pl.BlockSpec(memory_space=pltpu.HBM)] * in_hbm} if in_hbm else {}
    return pl.pallas_call(
        kernel,
        out_shape=outs if single else tuple(outs),
        scratch_shapes=list(scratch),
        **extra,
        compiler_params=pltpu.CompilerParams(vmem_limit_bytes=limit * 1024 * 1024),
        cost_estimate=pl.CostEstimate(
            flops=flops, bytes_accessed=bytes_accessed, transcendentals=0
        ),
    )


def f32(*shape):
    return jax.ShapeDtypeStruct(shape, jnp.float32)


def swapped(shard, axis, start):
    pairs = []
    for i in range(start, lax.axis_size(axis) - 1, 2):
        pairs += [(i, i + 1), (i + 1, i)]
    return lax.ppermute(shard, axis, pairs)


def body(rhs, viscosity, cell_mask, friction, stiffness):
    devices = lax.axis_size("rx") * lax.axis_size("ry")
    natural = [
        pltpu.with_memory_space_constraint(x, pltpu.HBM)
        for x in (rhs.reshape(22, 8, 512), viscosity, cell_mask, friction)
    ]
    first, second, *local = call(
        rows_kernel,
        (f32(DEPTH, 48, 512), f32(DEPTH, 48, 512), f32(22, 8, 512), f32(10, 2, 8, 512),
         jax.ShapeDtypeStruct((8, 512), jnp.int32), f32(8, 512)),
        [pltpu.VMEM((2, 48, 512), jnp.float32), pltpu.SemaphoreType.DMA((4,))],
        bytes_accessed=10**6,
        in_hbm=4,
    )(*natural)
    first_rows = swapped(first, "rx", 0)
    second_rows = swapped(second, "rx", 1)
    own, packs, weights, *prepared = call(
        own_kernel,
        (
            f32(8, 48, LANES),
            f32(48, EDGE),
            jax.ShapeDtypeStruct((2, GROUPS, 3 * HALF), jnp.bfloat16),
            f32(8, 96, LANES),
            f32(8, 24, LANES),
            f32(3, 8, 24, LANES),
            jax.ShapeDtypeStruct((3, 2, BLOCK, LANES), jnp.bfloat16),
            f32(3, 24, LANES),
            f32(3, 2, 24, LANES),
        ),
        [pltpu.VMEM((2, 8 * BLOCK, LANES), jnp.bfloat16)],
        flops=10**9,
        bytes_accessed=10**6,
        limit=16,
    )(*local, stiffness)
    inner = prepared[2]
    packs = call(cols_kernel, f32(48, EDGE), bytes_accessed=10**6)(packs, first_rows, second_rows)
    first_cols = swapped(packs, "ry", 0)
    second_cols = swapped(packs, "ry", 1)
    outer, line = call(
        main_kernel,
        (f32(3, 8, 24, LANES), f32(8, 128)),
        [
            pltpu.VMEM((NROW - 1, 96, LANES), jnp.float32),
            pltpu.VMEM((NROW, 24, LANES), jnp.float32),
            pltpu.VMEM((4, NROW, 24, LANES), jnp.float32),
            pltpu.VMEM((2, NROW * BLOCK, LANES), jnp.bfloat16),
        ],
        flops=2 * 10**9,
        bytes_accessed=3 * 10**6,
        limit=24,
    )(own, weights, *prepared, first_rows, second_rows, stiffness)
    edges, gram = call(
        edge_kernel,
        (f32(4, 24, EDGE), f32(devices, 128)),
        [pltpu.VMEM((96, EDGE), jnp.float32)],
        flops=10**8,
        bytes_accessed=10**6,
    )(packs, first_cols, second_cols, stiffness, weights, line)
    grams = lax.all_to_all(gram.reshape(devices, 1, 128), ("rx", "ry"), 0, 0)
    update, last = call(combine_kernel, (f32(22, 8, 512),) * 2, bytes_accessed=3 * 10**6)(
        own, inner, outer, edges, grams.reshape(devices, 128), stiffness
    )
    return update.reshape(2, 11, 8, 512), last.reshape(2, 11, 8, 512)


def solution(mesh):
    in_specs = (
        P(None, None, "rx", "ry"),
        P(None, None, "rx", "ry"),
        P("rx", "ry"),
        P("rx", "ry"),
        P(),
    )
    out_specs = (P(None, None, "rx", "ry"), P(None, None, "rx", "ry"))
    return jax.shard_map(body, mesh=mesh, in_specs=in_specs, out_specs=out_specs, check_vma=False)
```

```python
import jax
import jax.numpy as jnp
from jax import lax
from jax.experimental import pallas as pl
from jax.experimental.pallas import tpu as pltpu
from jax.sharding import PartitionSpec as P


DEPTH = 3
NROW = 8 + 2 * DEPTH
LANES = 512
PITCH = 18
EDGE = 256
PAIRS = [(a, b) for a in range(4) for b in range(a, 4)]
HALF = 80
BLOCK = 2 * HALF
GROUPS = 144


def shift_of(stiff):
    rows = lax.broadcasted_iota(jnp.int32, (12, 12), 0)
    cols = lax.broadcasted_iota(jnp.int32, (12, 12), 1)
    trace = jnp.sum(jnp.where(rows == cols, stiff[:, 0, :] + stiff[:, 1, :], 0.0))
    return 1.0 + trace * (1.2 * 10.0 / 22.0)


def own_row(out, rhs, visc, mask, fric, row):
    ice = mask[row : row + 1, :].astype(jnp.float32)
    out[0:22, 0:512] = rhs[:, row, :]
    out[22:23, 0:512] = jnp.ones_like(ice)
    out[23:24, 0:512] = fric[row : row + 1, :]
    out[24:34, 0:512] = visc[:, 0, row, :] * ice
    out[34:44, 0:512] = visc[:, 1, row, :] * ice
    out[44:48, 0:512] = jnp.zeros((4, 512), jnp.float32)


def odd_along(axis):
    return lax.rem(lax.axis_index(axis), 2) == 1


def rows_kernel(
    rhs, visc, mask, fric, stiff,
    first, second, rhs_out, visc_out, mask_out, fric_out, stiff_out,
    work, sems,
):
    sources = (rhs, visc, mask, fric, stiff)
    targets = (rhs_out, visc_out, mask_out, fric_out, stiff_out)
    copies = [
        pltpu.make_async_copy(src, dst, sems.at[n])
        for n, (src, dst) in enumerate(zip(sources, targets))
    ]
    for copy in copies:
        copy.start()
    for copy in copies:
        copy.wait()
    odd = odd_along("rx")
    for j in range(DEPTH):
        own_row(work.at[0], rhs_out, visc_out, mask_out, fric_out, 8 - DEPTH + j)
        own_row(work.at[1], rhs_out, visc_out, mask_out, fric_out, j)
        up, down = (work[0], work[1])
        first[j] = jnp.where(odd, down, up)
        second[j] = jnp.where(odd, up, down)


def pack_kernel(rhs, visc, mask, fric, packs):
    lane = lax.broadcasted_iota(jnp.int32, (48, EDGE), 1)
    packed = jnp.zeros((48, EDGE), jnp.float32)

    def ends(rows):
        return jnp.concatenate([rows[..., 0:128], rows[..., 384:512]], axis=-1)

    for r in range(8):
        ice = ends(mask[r : r + 1, :]).astype(jnp.float32)
        row = jnp.concatenate(
            [
                ends(rhs[:, r, :]),
                jnp.ones_like(ice),
                ends(fric[r : r + 1, :]),
                ends(visc[:, 0, r, :]) * ice,
                ends(visc[:, 1, r, :]) * ice,
                jnp.zeros((4, EDGE), jnp.float32),
            ],
            axis=0,
        )
        start = PITCH * (r + DEPTH)
        at = lane - start
        packed = jnp.where((at >= 0) & (at < 9), pltpu.roll(row, (start + 3) % EDGE, 1), packed)
        packed = jnp.where((at >= 9) & (at < 18), pltpu.roll(row, (start + 15) % EDGE, 1), packed)
    packs[...] = packed


def corners_kernel(packs, first_cols, second_cols, out):
    odd_col = odd_along("ry")
    at = lax.rem(lax.broadcasted_iota(jnp.int32, (48, EDGE), 1), PITCH)
    from_left = jnp.where(odd_col, first_cols[...], second_cols[...])
    from_right = jnp.where(odd_col, second_cols[...], first_cols[...])
    out[...] = jnp.where(at < 3, from_left, jnp.where(at >= 15, from_right, packs[...]))


def weights_kernel(stiff, weights):
    row = lax.broadcasted_iota(jnp.int32, (GROUPS, 12), 0)
    col = lax.broadcasted_iota(jnp.int32, (GROUPS, 12), 1)

    def of_row(r):
        group, plane = (r // 24, r % 24)
        slot, lev = (group // 2, group % 2)
        comp, level = (plane // 11, plane % 11)
        layer = level - lev
        good = (plane < 22) & (layer >= 0) & (layer < 10)
        return comp * 6 + lev * 3 + slot, layer, good

    pick = jnp.where(of_row(row)[0] == col, 1.0, 0.0)
    r = lax.broadcasted_iota(jnp.int32, (GROUPS, 3 * HALF), 0)
    k = lax.broadcasted_iota(jnp.int32, (GROUPS, 3 * HALF), 1)
    _, layer, good = of_row(r)
    part = (k % HALF) // 24
    plane = (k % HALF) % 24
    lev_in = plane % 11 - layer
    good = good & (part < 3) & (plane < 22)
    q = lax.broadcasted_iota(jnp.int32, (12, 3 * HALF), 0)
    kq = lax.broadcasted_iota(jnp.int32, (12, 3 * HALF), 1)
    comp_in = ((kq % HALF) % 24) // 11
    block = kq // HALF
    for tri in range(2):
        first, second, third = ((0, 2, 1), (2, 0, 1))[tri]
        place = jnp.where(block == 0, first, jnp.where(block == 1, second, third))
        rows = jnp.dot(
            pick, stiff[:, tri, :], precision=lax.Precision.HIGHEST, preferred_element_type=jnp.float32
        )
        total = jnp.zeros((GROUPS, 3 * HALF), jnp.float32)
        for lev in range(2):
            sel = jnp.where(comp_in * 6 + lev * 3 + place == q, 1.0, 0.0)
            spread = jnp.dot(
                rows, sel, precision=lax.Precision.HIGHEST, preferred_element_type=jnp.float32
            )
            total = jnp.where(good & (lev_in == lev), spread, total)
        high = total.astype(jnp.bfloat16).astype(jnp.float32)
        weights[tri] = jnp.where(part == 2, total - high, high).astype(jnp.bfloat16)


def split_rows(x):
    high = x.astype(jnp.bfloat16).astype(jnp.float32)
    pad = jnp.zeros((HALF - 72, x.shape[1]), jnp.float32)
    return jnp.concatenate([high, x - high, high, pad], axis=0).astype(jnp.bfloat16)


def put_operand(operand, i, x):
    operand[i * BLOCK : i * BLOCK + HALF, :] = split_rows(x)
    operand[i * BLOCK + HALF : (i + 1) * BLOCK, :] = split_rows(pltpu.roll(x, LANES - 1, 1))


def put_scale(out, coefs):
    zeros = jnp.zeros((24, out.shape[1]), jnp.float32)
    for tri in range(2):
        for lev in range(2):
            base = 48 * tri + 24 * lev
            out[base : base + 24, :] = zeros
            out[base + lev : base + lev + 10, :] = coefs[tri]
            out[base + 11 + lev : base + 21 + lev, :] = coefs[tri]


def grown_of(scale, mixed):
    parts = []
    for tri in range(2):
        upper = scale[48 * tri : 48 * tri + 24, :]
        lower = scale[48 * tri + 24 : 48 * tri + 48, :]
        for slot in range(3):
            at = 48 * slot
            parts.append(upper * mixed[tri][at : at + 24] + lower * mixed[tri][at + 24 : at + 48])
    return parts[0], parts[1] + parts[3], parts[2] + parts[5], parts[4]


def inner_products(vectors, sums, lanes):
    result = []
    for total, (a, b) in zip(sums, PAIRS):
        product = vectors[a] * vectors[b]
        for s in range(0, 24, 8):
            for l in range(0, lanes, 128):
                total = total + product[s : s + 8, l : l + 128]
        result.append(total)
    return tuple(result)


def line_of(sums):
    place = lax.broadcasted_iota(jnp.int32, (8, 128), 1)
    line = jnp.zeros((8, 128), jnp.float32)
    for n, total in enumerate(sums):
        line = jnp.where(place == n, jnp.sum(total), line)
    return line


def no_sums():
    return tuple(jnp.zeros((8, 128), jnp.float32) for _ in PAIRS)


def products(weights, source, i):
    start = i * BLOCK
    return [
        jnp.dot(
            weights[tri],
            source[start + HALF * tri : start + HALF * (tri + 3), :],
            preferred_element_type=jnp.float32,
        )
        for tri in range(2)
    ]


def bottom_planes(lanes):
    plane = lax.broadcasted_iota(jnp.int32, (24, lanes), 0)
    return (plane == 0) | (plane == 11)


def field_planes(row):
    plane = lax.broadcasted_iota(jnp.int32, (24, row.shape[1]), 0)
    return jnp.where(plane < 22, row[0:24, :], 0.0)


def diag_planes(row, theta):
    on_bottom = jnp.where(bottom_planes(row.shape[1]), row[23:24, :], 0.0)
    return row[22:23, :] * (1.0 - theta) + on_bottom


def is_inner(k, i):
    return DEPTH + k <= i <= DEPTH + 7 - k


def own_kernel(
    rhs, visc, mask, fric, stiff,
    own, weights, scale, diag, powers, bounds, low_parts, high_parts,
    operand,
):
    weights_kernel(stiff, weights)
    theta = shift_of(stiff)
    for r in range(8):
        own_row(own.at[r], rhs, visc, mask, fric, r)
        row = own[r]
        put_operand(operand.at[0], r, field_planes(row))
        diag[r] = diag_planes(row, theta)
        put_scale(scale.at[r], (row[24:34, :], row[34:44, :]))
    for step in range(1, DEPTH + 1):
        source = operand.at[(step - 1) % 2]
        target = operand.at[step % 2]
        first, last = (step - 1, 8 - step)
        bounds[step - 1, 0] = source[first * BLOCK : (first + 1) * BLOCK, :]
        bounds[step - 1, 1] = source[last * BLOCK : (last + 1) * BLOCK, :]
        for r in range(first, last):
            a, b, c, d = grown_of(scale[r], products(weights, source, r))
            if r == first:
                low_parts[step - 1] = a + pltpu.roll(c, 1, 1)
            else:
                total = a + upper + pltpu.roll(c + across, 1, 1)
                before = powers[step - 2, r] if step > 1 else field_planes(own[r])
                x = total + diag[r] * before
                powers[step - 1, r] = x
                if step < DEPTH:
                    put_operand(target, r, x)
            upper, across = (b, d)
        high_parts[step - 1, 0] = upper
        high_parts[step - 1, 1] = across


def main_kernel(
    own, weights, own_scale, own_diag, inner, bounds, low_parts, high_parts, first_rows, second_rows, stiff,
    outer, line,
    scale, diag, field, operand,
):
    odd_row = odd_along("rx")
    theta = shift_of(stiff)
    real = {}
    for i in (0, 1, 2, 11, 12, 13):
        if i < DEPTH:
            row = jnp.where(odd_row, first_rows[i], second_rows[i])
        else:
            j = i - 8 - DEPTH
            row = jnp.where(odd_row, second_rows[j], first_rows[j])
            real[i] = row[22:23, :]
        x = field_planes(row)
        field[0, i] = x
        put_operand(operand.at[0], i, x)
        diag[i] = diag_planes(row, theta)
        if i < NROW - 1:
            put_scale(scale.at[i], (row[24:34, :], row[34:44, :]))

    def power(k, i):
        if k == 0 and is_inner(0, i):
            return field_planes(own[i - DEPTH])
        return inner[k - 1, i - DEPTH] if is_inner(k, i) else field[k, i]

    for step in range(1, DEPTH + 1):
        source = operand.at[(step - 1) % 2]
        target = operand.at[step % 2]
        for side, i in ((0, DEPTH + step - 1), (1, DEPTH + 8 - step)):
            source[i * BLOCK : (i + 1) * BLOCK, :] = bounds[step - 1, side]

        def grown(i, source=source):
            is_own = is_inner(0, i)
            return grown_of(own_scale[i - DEPTH] if is_own else scale[i], products(weights, source, i))

        def put(i, total, step=step, target=target):
            if i in real:
                total = total * real[i]
            x = total + (own_diag[i - DEPTH] if is_inner(0, i) else diag[i]) * power(step - 1, i)
            field[step, i] = x
            if is_inner(0, i):
                outer[step - 1, i - DEPTH] = x
            if step < DEPTH:
                put_operand(target, i, x)

        first = step - 1
        _, upper, _, across = grown(first)
        for i in range(first + 1, first + 3):
            a, b, c, d = grown(i)
            put(i, a + upper + pltpu.roll(c + across, 1, 1))
            upper, across = (b, d)
        put(first + 3, low_parts[step - 1] + upper + pltpu.roll(across, 1, 1))
        upper, across = (high_parts[step - 1, 0], high_parts[step - 1, 1])
        for i in range(11 - step, 14 - step):
            a, b, c, d = grown(i)
            put(i, a + upper + pltpu.roll(c + across, 1, 1))
            upper, across = (b, d)

    lane = lax.broadcasted_iota(jnp.int32, (24, LANES), 1)
    inside = (lane >= DEPTH) & (lane < LANES - DEPTH)
    sums = no_sums()
    for r in range(8):
        vectors = [jnp.where(inside, power(a, r + DEPTH), 0.0) for a in range(4)]
        sums = inner_products(vectors, sums, LANES)
    line[...] = line_of(sums)


def edge_kernel(cols, first_rows, second_rows, stiff, weights, line, edges, gram, scale):
    odd_row = odd_along("rx")
    theta = shift_of(stiff)
    lane = lax.broadcasted_iota(jnp.int32, (48, EDGE), 1)
    low = jnp.where(odd_row, first_rows[...], second_rows[...])
    high = jnp.where(odd_row, second_rows[...], first_rows[...])
    full = jnp.where(lane < PITCH * DEPTH, pltpu.roll(low, EDGE - 8 * PITCH, 1), cols[...])
    full = jnp.where(lane >= PITCH * (8 + DEPTH), pltpu.roll(high, 8 * PITCH, 1), full)
    put_scale(scale, (full[24:34], full[34:44]))
    real = full[22:23]
    diag = diag_planes(full, theta)
    x = field_planes(full)
    vectors = [x]
    for _ in range(DEPTH):
        corners = [
            split_rows(pltpu.roll(x, (EDGE - by) % EDGE, 1) if by else x)
            for by in (0, 1, PITCH, PITCH + 1)
        ]
        mixed = [
            jnp.dot(
                weights[tri],
                jnp.concatenate(corners[tri : tri + 3], axis=0),
                preferred_element_type=jnp.float32,
            )
            for tri in range(2)
        ]
        a, b, c, d = grown_of(scale[...], mixed)
        total = a + pltpu.roll(b, PITCH, 1) + pltpu.roll(c + pltpu.roll(d, PITCH, 1), 1, 1)
        x = real * total + diag * x
        vectors.append(x)
    for a in range(4):
        edges[a] = vectors[a]
    lane = lax.broadcasted_iota(jnp.int32, (24, EDGE), 1)
    at = lax.rem(lane, PITCH)
    mine = (lane >= PITCH * DEPTH) & (lane < PITCH * (DEPTH + 8))
    mine = mine & (((at >= 3) & (at < 6)) | ((at >= 12) & (at < 15)))
    sums = inner_products([jnp.where(mine, v, 0.0) for v in vectors], no_sums(), EDGE)
    total = line[...] + line_of(sums)
    gram[...] = jnp.broadcast_to(total[0:1], gram.shape)


def combine_kernel(own, inner, outer, edges, grams, stiff, update, last):
    theta = shift_of(stiff)
    entry = jnp.sum(grams[...], axis=0, keepdims=True)
    place = lax.broadcasted_iota(jnp.int32, (1, 128), 1)
    g = {}
    for n, pair in enumerate(PAIRS):
        g[pair] = jnp.sum(jnp.where(place == n, entry, 0.0), axis=1, keepdims=True)
    upper = [[None] * 4 for _ in range(4)]
    for a in range(4):
        for b in range(a, 4):
            value = g[a, b]
            for c in range(a):
                value = value - upper[c][a] * upper[c][b]
            if a == b:
                upper[a][a] = jnp.sqrt(value)
            else:
                upper[a][b] = value / upper[a][a]
    zero = jnp.zeros((1, 1), jnp.float32)
    table = [
        [
            (upper[a][b + 1] if a <= b + 1 else zero) + (theta * upper[a][b] if a <= b else zero)
            for b in range(3)
        ]
        for a in range(4)
    ]
    target = [upper[0][0], zero, zero, zero]
    for col in range(3):
        first, second = (table[col][col], table[col + 1][col])
        radius = jnp.sqrt(first * first + second * second)
        cosine, sine = (first / radius, second / radius)
        for c in range(col, 3):
            one, two = (table[col][c], table[col + 1][c])
            table[col][c] = cosine * one + sine * two
            table[col + 1][c] = cosine * two - sine * one
        one, two = (target[col], target[col + 1])
        target[col] = cosine * one + sine * two
        target[col + 1] = cosine * two - sine * one
    z = [None] * 3
    for col in (2, 1, 0):
        value = target[col]
        for c in range(col + 1, 3):
            value = value - table[col][c] * z[c]
        z[col] = value / table[col][col]
    w = [None] * 4
    w[3] = 1.0 / upper[3][3]
    for a in (2, 1, 0):
        value = zero
        for c in range(a + 1, 4):
            value = value - upper[a][c] * w[c]
        w[a] = value / upper[a][a]
    lane = lax.broadcasted_iota(jnp.int32, (22, 128), 1)
    for out, factors in ((update, z), (last, w)):
        ends = factors[0] * edges[0]
        for a in range(1, len(factors)):
            ends = ends + factors[a] * edges[a]
        for r in range(8):
            row = factors[0] * own[r, 0:22, :]
            for a in range(1, len(factors)):
                part = inner if is_inner(a, r + DEPTH) else outer
                row = row + factors[a] * part[a - 1, r, 0:22, :]
            at = PITCH * (r + DEPTH)
            left = pltpu.roll(ends, (EDGE - at - 3) % EDGE, 1)[0:22, 0:128]
            right = pltpu.roll(ends, (253 - at - 12) % EDGE, 1)[0:22, 128:256]
            out[:, r, 0:128] = jnp.where(lane < DEPTH, left, row[:, 0:128])
            out[:, r, 128:384] = row[:, 128:384]
            out[:, r, 384:512] = jnp.where(lane >= 128 - DEPTH, right, row[:, 384:512])


def call(kernel, outs, scratch=(), flops=0, bytes_accessed=0, limit=8, in_hbm=0):
    single = not isinstance(outs, (list, tuple))
    extra = {"in_specs": [pl.BlockSpec(memory_space=pltpu.HBM)] * in_hbm} if in_hbm else {}
    return pl.pallas_call(
        kernel,
        out_shape=outs if single else tuple(outs),
        scratch_shapes=list(scratch),
        **extra,
        compiler_params=pltpu.CompilerParams(vmem_limit_bytes=limit * 1024 * 1024),
        cost_estimate=pl.CostEstimate(
            flops=flops, bytes_accessed=bytes_accessed, transcendentals=0
        ),
    )


def f32(*shape):
    return jax.ShapeDtypeStruct(shape, jnp.float32)


def swapped(shard, axis, start):
    pairs = []
    for i in range(start, lax.axis_size(axis) - 1, 2):
        pairs += [(i, i + 1), (i + 1, i)]
    return lax.ppermute(shard, axis, pairs)


def body(rhs, viscosity, cell_mask, friction, stiffness):
    devices = lax.axis_size("rx") * lax.axis_size("ry")
    natural = [
        pltpu.with_memory_space_constraint(x, pltpu.HBM)
        for x in (rhs.reshape(22, 8, 512), viscosity, cell_mask, friction, stiffness.transpose(1, 0, 2))
    ]
    first, second, *local, stiff = call(
        rows_kernel,
        (f32(DEPTH, 48, 512), f32(DEPTH, 48, 512), f32(22, 8, 512), f32(10, 2, 8, 512),
         jax.ShapeDtypeStruct((8, 512), jnp.int32), f32(8, 512), f32(12, 2, 12)),
        [pltpu.VMEM((2, 48, 512), jnp.float32), pltpu.SemaphoreType.DMA((5,))],
        bytes_accessed=10**6,
        in_hbm=5,
    )(*natural)
    first_rows = swapped(first, "rx", 0)
    second_rows = swapped(second, "rx", 1)
    packs = call(pack_kernel, f32(48, EDGE), bytes_accessed=10**5)(*local)
    first_cols = swapped(packs, "ry", 0)
    second_cols = swapped(packs, "ry", 1)
    own, weights, *prepared = call(
        own_kernel,
        (
            f32(8, 48, LANES),
            jax.ShapeDtypeStruct((2, GROUPS, 3 * HALF), jnp.bfloat16),
            f32(8, 96, LANES),
            f32(8, 24, LANES),
            f32(3, 8, 24, LANES),
            jax.ShapeDtypeStruct((3, 2, BLOCK, LANES), jnp.bfloat16),
            f32(3, 24, LANES),
            f32(3, 2, 24, LANES),
        ),
        [pltpu.VMEM((2, 8 * BLOCK, LANES), jnp.bfloat16)],
        flops=10**9,
        bytes_accessed=10**6,
        limit=16,
    )(*local, stiff)
    inner = prepared[2]
    cols = call(corners_kernel, f32(48, EDGE), bytes_accessed=10**5)(packs, first_cols, second_cols)
    first_corners = swapped(cols, "rx", 0)
    second_corners = swapped(cols, "rx", 1)
    outer, line = call(
        main_kernel,
        (f32(3, 8, 24, LANES), f32(8, 128)),
        [
            pltpu.VMEM((NROW - 1, 96, LANES), jnp.float32),
            pltpu.VMEM((NROW, 24, LANES), jnp.float32),
            pltpu.VMEM((4, NROW, 24, LANES), jnp.float32),
            pltpu.VMEM((2, NROW * BLOCK, LANES), jnp.bfloat16),
        ],
        flops=2 * 10**9,
        bytes_accessed=3 * 10**6,
        limit=24,
    )(own, weights, *prepared, first_rows, second_rows, stiff)
    edges, gram = call(
        edge_kernel,
        (f32(4, 24, EDGE), f32(devices, 128)),
        [pltpu.VMEM((96, EDGE), jnp.float32)],
        flops=10**8,
        bytes_accessed=10**6,
    )(cols, first_corners, second_corners, stiff, weights, line)
    grams = lax.all_to_all(gram.reshape(devices, 1, 128), ("rx", "ry"), 0, 0)
    update, last = call(combine_kernel, (f32(22, 8, 512),) * 2, bytes_accessed=3 * 10**6)(
        own, inner, outer, edges, grams.reshape(devices, 128), stiff
    )
    return update.reshape(2, 11, 8, 512), last.reshape(2, 11, 8, 512)


def solution(mesh):
    in_specs = (
        P(None, None, "rx", "ry"),
        P(None, None, "rx", "ry"),
        P("rx", "ry"),
        P("rx", "ry"),
        P(),
    )
    out_specs = (P(None, None, "rx", "ry"), P(None, None, "rx", "ry"))
    return jax.shard_map(body, mesh=mesh, in_specs=in_specs, out_specs=out_specs, check_vma=False)
```

```python
import jax
import jax.numpy as jnp
from jax import lax
from jax.experimental import pallas as pl
from jax.experimental.pallas import tpu as pltpu
from jax.sharding import PartitionSpec as P


DEPTH = 3
NROW = 8 + 2 * DEPTH
LANES = 512
PITCH = 18
EDGE = 256
PAIRS = [(a, b) for a in range(4) for b in range(a, 4)]
HALF = 80
BLOCK = 2 * HALF
GROUPS = 144


def shift_of(stiff):
    rows = lax.broadcasted_iota(jnp.int32, (12, 12), 0)
    cols = lax.broadcasted_iota(jnp.int32, (12, 12), 1)
    trace = jnp.sum(jnp.where(rows == cols, stiff[:, 0, :] + stiff[:, 1, :], 0.0))
    return 1.0 + trace * (1.2 * 10.0 / 22.0)


def own_row(out, rhs, visc, mask, fric, row):
    ice = mask[row : row + 1, :].astype(jnp.float32)
    out[0:22, 0:512] = rhs[:, row, :]
    out[22:23, 0:512] = jnp.ones_like(ice)
    out[23:24, 0:512] = fric[row : row + 1, :]
    out[24:34, 0:512] = visc[:, 0, row, :] * ice
    out[34:44, 0:512] = visc[:, 1, row, :] * ice
    out[44:48, 0:512] = jnp.zeros((4, 512), jnp.float32)


def odd_along(axis):
    return lax.rem(lax.axis_index(axis), 2) == 1


def rows_kernel(
    rhs, visc, mask, fric, stiff,
    first, second, rhs_out, visc_out, mask_out, fric_out, stiff_out,
    work, sems,
):
    sources = (rhs, visc, mask, fric, stiff)
    targets = (rhs_out, visc_out, mask_out, fric_out, stiff_out)
    copies = [
        pltpu.make_async_copy(src, dst, sems.at[n])
        for n, (src, dst) in enumerate(zip(sources, targets))
    ]
    for copy in copies:
        copy.start()
    for copy in copies:
        copy.wait()
    odd = odd_along("rx")
    for j in range(DEPTH):
        own_row(work.at[0], rhs_out, visc_out, mask_out, fric_out, 8 - DEPTH + j)
        own_row(work.at[1], rhs_out, visc_out, mask_out, fric_out, j)
        up, down = (work[0], work[1])
        first[j] = jnp.where(odd, down, up)
        second[j] = jnp.where(odd, up, down)


def pack_row(row, i, lane, packed):
    ends = jnp.concatenate([row[:, 0:128], row[:, 384:512]], axis=1)
    at = lane - PITCH * i
    packed = jnp.where((at >= 0) & (at < 9), pltpu.roll(ends, (PITCH * i + 3) % EDGE, 1), packed)
    return jnp.where((at >= 9) & (at < 18), pltpu.roll(ends, (PITCH * i + 15) % EDGE, 1), packed)


def cols_kernel(packs, first_rows, second_rows, out):
    odd_row = odd_along("rx")
    lane = lax.broadcasted_iota(jnp.int32, (48, EDGE), 1)
    packed = packs[...]
    for j in range(DEPTH):
        one, two = (first_rows[j], second_rows[j])
        packed = pack_row(jnp.where(odd_row, one, two), j, lane, packed)
        packed = pack_row(jnp.where(odd_row, two, one), j + 8 + DEPTH, lane, packed)
    out[...] = packed


def weights_kernel(stiff, weights):
    row = lax.broadcasted_iota(jnp.int32, (GROUPS, 12), 0)
    col = lax.broadcasted_iota(jnp.int32, (GROUPS, 12), 1)

    def of_row(r):
        group, plane = (r // 24, r % 24)
        slot, lev = (group // 2, group % 2)
        comp, level = (plane // 11, plane % 11)
        layer = level - lev
        good = (plane < 22) & (layer >= 0) & (layer < 10)
        return comp * 6 + lev * 3 + slot, layer, good

    pick = jnp.where(of_row(row)[0] == col, 1.0, 0.0)
    r = lax.broadcasted_iota(jnp.int32, (GROUPS, 3 * HALF), 0)
    k = lax.broadcasted_iota(jnp.int32, (GROUPS, 3 * HALF), 1)
    _, layer, good = of_row(r)
    part = (k % HALF) // 24
    plane = (k % HALF) % 24
    lev_in = plane % 11 - layer
    good = good & (part < 3) & (plane < 22)
    q = lax.broadcasted_iota(jnp.int32, (12, 3 * HALF), 0)
    kq = lax.broadcasted_iota(jnp.int32, (12, 3 * HALF), 1)
    comp_in = ((kq % HALF) % 24) // 11
    block = kq // HALF
    for tri in range(2):
        first, second, third = ((0, 2, 1), (2, 0, 1))[tri]
        place = jnp.where(block == 0, first, jnp.where(block == 1, second, third))
        rows = jnp.dot(
            pick, stiff[:, tri, :], precision=lax.Precision.HIGHEST, preferred_element_type=jnp.float32
        )
        total = jnp.zeros((GROUPS, 3 * HALF), jnp.float32)
        for lev in range(2):
            sel = jnp.where(comp_in * 6 + lev * 3 + place == q, 1.0, 0.0)
            spread = jnp.dot(
                rows, sel, precision=lax.Precision.HIGHEST, preferred_element_type=jnp.float32
            )
            total = jnp.where(good & (lev_in == lev), spread, total)
        high = total.astype(jnp.bfloat16).astype(jnp.float32)
        weights[tri] = jnp.where(part == 2, total - high, high).astype(jnp.bfloat16)


def split_rows(x):
    high = x.astype(jnp.bfloat16).astype(jnp.float32)
    pad = jnp.zeros((HALF - 72, x.shape[1]), jnp.float32)
    return jnp.concatenate([high, x - high, high, pad], axis=0).astype(jnp.bfloat16)


def put_operand(operand, i, x):
    operand[i * BLOCK : i * BLOCK + HALF, :] = split_rows(x)
    operand[i * BLOCK + HALF : (i + 1) * BLOCK, :] = split_rows(pltpu.roll(x, LANES - 1, 1))


def put_scale(out, coefs):
    zeros = jnp.zeros((24, out.shape[1]), jnp.float32)
    for tri in range(2):
        for lev in range(2):
            base = 48 * tri + 24 * lev
            out[base : base + 24, :] = zeros
            out[base + lev : base + lev + 10, :] = coefs[tri]
            out[base + 11 + lev : base + 21 + lev, :] = coefs[tri]


def grown_of(scale, mixed):
    parts = []
    for tri in range(2):
        upper = scale[48 * tri : 48 * tri + 24, :]
        lower = scale[48 * tri + 24 : 48 * tri + 48, :]
        for slot in range(3):
            at = 48 * slot
            parts.append(upper * mixed[tri][at : at + 24] + lower * mixed[tri][at + 24 : at + 48])
    return parts[0], parts[1] + parts[3], parts[2] + parts[5], parts[4]


def inner_products(vectors, sums, lanes):
    result = []
    for total, (a, b) in zip(sums, PAIRS):
        product = vectors[a] * vectors[b]
        for s in range(0, 24, 8):
            for l in range(0, lanes, 128):
                total = total + product[s : s + 8, l : l + 128]
        result.append(total)
    return tuple(result)


def line_of(sums):
    rows = [jnp.sum(total, axis=0, keepdims=True) for total in sums]
    rows.append(jnp.zeros((16 - len(rows), 128), jnp.float32))
    totals = jnp.sum(jnp.concatenate(rows, axis=0), axis=1, keepdims=True)
    row = lax.broadcasted_iota(jnp.int32, (16, 128), 0)
    place = lax.broadcasted_iota(jnp.int32, (16, 128), 1)
    line = jnp.sum(jnp.where(place == row, totals, 0.0), axis=0, keepdims=True)
    return jnp.broadcast_to(line, (8, 128))


def no_sums():
    return tuple(jnp.zeros((8, 128), jnp.float32) for _ in PAIRS)


def products(weights, source, i):
    start = i * BLOCK
    return [
        jnp.dot(
            weights[tri],
            source[start + HALF * tri : start + HALF * (tri + 3), :],
            preferred_element_type=jnp.float32,
        )
        for tri in range(2)
    ]


def bottom_planes(lanes):
    plane = lax.broadcasted_iota(jnp.int32, (24, lanes), 0)
    return (plane == 0) | (plane == 11)


def field_planes(row):
    plane = lax.broadcasted_iota(jnp.int32, (24, row.shape[1]), 0)
    return jnp.where(plane < 22, row[0:24, :], 0.0)


def diag_planes(row, theta):
    on_bottom = jnp.where(bottom_planes(row.shape[1]), row[23:24, :], 0.0)
    return row[22:23, :] * (1.0 - theta) + on_bottom


def is_inner(k, i):
    return DEPTH + k <= i <= DEPTH + 7 - k


def own_kernel(
    rhs, visc, mask, fric, stiff,
    own, packs, weights, scale, diag, powers, bounds, low_parts, high_parts,
    operand,
):
    weights_kernel(stiff, weights)
    theta = shift_of(stiff)
    lane = lax.broadcasted_iota(jnp.int32, (48, EDGE), 1)
    packed = jnp.zeros((48, EDGE), jnp.float32)
    for r in range(8):
        own_row(own.at[r], rhs, visc, mask, fric, r)
        row = own[r]
        packed = pack_row(row, r + DEPTH, lane, packed)
        put_operand(operand.at[0], r, field_planes(row))
        diag[r] = diag_planes(row, theta)
        put_scale(scale.at[r], (row[24:34, :], row[34:44, :]))
    packs[...] = packed
    for step in range(1, DEPTH + 1):
        source = operand.at[(step - 1) % 2]
        target = operand.at[step % 2]
        first, last = (step - 1, 8 - step)
        bounds[step - 1, 0] = source[first * BLOCK : (first + 1) * BLOCK, :]
        bounds[step - 1, 1] = source[last * BLOCK : (last + 1) * BLOCK, :]
        for r in range(first, last):
            a, b, c, d = grown_of(scale[r], products(weights, source, r))
            if r == first:
                low_parts[step - 1] = a + pltpu.roll(c, 1, 1)
            else:
                total = a + upper + pltpu.roll(c + across, 1, 1)
                before = powers[step - 2, r] if step > 1 else field_planes(own[r])
                x = total + diag[r] * before
                powers[step - 1, r] = x
                if step < DEPTH:
                    put_operand(target, r, x)
            upper, across = (b, d)
        high_parts[step - 1, 0] = upper
        high_parts[step - 1, 1] = across


def main_kernel(
    own, weights, own_scale, own_diag, inner, bounds, low_parts, high_parts, first_rows, second_rows, stiff,
    outer, line,
    scale, diag, field, operand,
):
    odd_row = odd_along("rx")
    theta = shift_of(stiff)
    real = {}
    for i in (0, 1, 2, 11, 12, 13):
        if i < DEPTH:
            row = jnp.where(odd_row, first_rows[i], second_rows[i])
        else:
            j = i - 8 - DEPTH
            row = jnp.where(odd_row, second_rows[j], first_rows[j])
            real[i] = row[22:23, :]
        x = field_planes(row)
        field[0, i] = x
        put_operand(operand.at[0], i, x)
        diag[i] = diag_planes(row, theta)
        if i < NROW - 1:
            put_scale(scale.at[i], (row[24:34, :], row[34:44, :]))

    def power(k, i):
        if k == 0 and is_inner(0, i):
            return field_planes(own[i - DEPTH])
        return inner[k - 1, i - DEPTH] if is_inner(k, i) else field[k, i]

    for step in range(1, DEPTH + 1):
        source = operand.at[(step - 1) % 2]
        target = operand.at[step % 2]
        for side, i in ((0, DEPTH + step - 1), (1, DEPTH + 8 - step)):
            source[i * BLOCK : (i + 1) * BLOCK, :] = bounds[step - 1, side]

        def grown(i, source=source):
            is_own = is_inner(0, i)
            return grown_of(own_scale[i - DEPTH] if is_own else scale[i], products(weights, source, i))

        def put(i, total, step=step, target=target):
            if i in real:
                total = total * real[i]
            x = total + (own_diag[i - DEPTH] if is_inner(0, i) else diag[i]) * power(step - 1, i)
            field[step, i] = x
            if is_inner(0, i):
                outer[step - 1, i - DEPTH] = x
            if step < DEPTH:
                put_operand(target, i, x)

        first = step - 1
        _, upper, _, across = grown(first)
        for i in range(first + 1, first + 3):
            a, b, c, d = grown(i)
            put(i, a + upper + pltpu.roll(c + across, 1, 1))
            upper, across = (b, d)
        put(first + 3, low_parts[step - 1] + upper + pltpu.roll(across, 1, 1))
        upper, across = (high_parts[step - 1, 0], high_parts[step - 1, 1])
        for i in range(11 - step, 14 - step):
            a, b, c, d = grown(i)
            put(i, a + upper + pltpu.roll(c + across, 1, 1))
            upper, across = (b, d)

    lane = lax.broadcasted_iota(jnp.int32, (24, LANES), 1)
    inside = (lane >= DEPTH) & (lane < LANES - DEPTH)
    sums = no_sums()
    for r in range(8):
        vectors = [jnp.where(inside, power(a, r + DEPTH), 0.0) for a in range(4)]
        sums = inner_products(vectors, sums, LANES)
    line[...] = line_of(sums)


def edge_kernel(packs, first_cols, second_cols, stiff, weights, line, edges, gram, scale):
    odd_col = odd_along("ry")
    theta = shift_of(stiff)
    at = lax.rem(lax.broadcasted_iota(jnp.int32, (48, EDGE), 1), PITCH)
    from_left = jnp.where(odd_col, first_cols[...], second_cols[...])
    from_right = jnp.where(odd_col, second_cols[...], first_cols[...])
    full = jnp.where(at < 3, from_left, jnp.where(at >= 15, from_right, packs[...]))
    put_scale(scale, (full[24:34], full[34:44]))
    real = full[22:23]
    diag = diag_planes(full, theta)
    x = field_planes(full)
    vectors = [x]
    for _ in range(DEPTH):
        corners = [
            split_rows(pltpu.roll(x, (EDGE - by) % EDGE, 1) if by else x)
            for by in (0, 1, PITCH, PITCH + 1)
        ]
        mixed = [
            jnp.dot(
                weights[tri],
                jnp.concatenate(corners[tri : tri + 3], axis=0),
                preferred_element_type=jnp.float32,
            )
            for tri in range(2)
        ]
        a, b, c, d = grown_of(scale[...], mixed)
        total = a + pltpu.roll(b, PITCH, 1) + pltpu.roll(c + pltpu.roll(d, PITCH, 1), 1, 1)
        x = real * total + diag * x
        vectors.append(x)
    for a in range(4):
        edges[a] = vectors[a]
    lane = lax.broadcasted_iota(jnp.int32, (24, EDGE), 1)
    at = lax.rem(lane, PITCH)
    mine = (lane >= PITCH * DEPTH) & (lane < PITCH * (DEPTH + 8))
    mine = mine & (((at >= 3) & (at < 6)) | ((at >= 12) & (at < 15)))
    sums = inner_products([jnp.where(mine, v, 0.0) for v in vectors], no_sums(), EDGE)
    total = line[...] + line_of(sums)
    gram[...] = jnp.broadcast_to(total[0:1], gram.shape)


def combine_kernel(own, inner, outer, edges, grams, stiff, update, last, parts, sems):
    theta = shift_of(stiff)
    entry = jnp.sum(grams[...], axis=0, keepdims=True)
    place = lax.broadcasted_iota(jnp.int32, (1, 128), 1)
    g = {}
    for n, pair in enumerate(PAIRS):
        g[pair] = jnp.sum(jnp.where(place == n, entry, 0.0), axis=1, keepdims=True)
    upper = [[None] * 4 for _ in range(4)]
    for a in range(4):
        for b in range(a, 4):
            value = g[a, b]
            for c in range(a):
                value = value - upper[c][a] * upper[c][b]
            if a == b:
                upper[a][a] = jnp.sqrt(value)
            else:
                upper[a][b] = value / upper[a][a]
    zero = jnp.zeros((1, 1), jnp.float32)
    table = [
        [
            (upper[a][b + 1] if a <= b + 1 else zero) + (theta * upper[a][b] if a <= b else zero)
            for b in range(3)
        ]
        for a in range(4)
    ]
    target = [upper[0][0], zero, zero, zero]
    for col in range(3):
        first, second = (table[col][col], table[col + 1][col])
        radius = jnp.sqrt(first * first + second * second)
        cosine, sine = (first / radius, second / radius)
        for c in range(col, 3):
            one, two = (table[col][c], table[col + 1][c])
            table[col][c] = cosine * one + sine * two
            table[col + 1][c] = cosine * two - sine * one
        one, two = (target[col], target[col + 1])
        target[col] = cosine * one + sine * two
        target[col + 1] = cosine * two - sine * one
    z = [None] * 3
    for col in (2, 1, 0):
        value = target[col]
        for c in range(col + 1, 3):
            value = value - table[col][c] * z[c]
        z[col] = value / table[col][col]
    w = [None] * 4
    w[3] = 1.0 / upper[3][3]
    for a in (2, 1, 0):
        value = zero
        for c in range(a + 1, 4):
            value = value - upper[a][c] * w[c]
        w[a] = value / upper[a][a]
    lane = lax.broadcasted_iota(jnp.int32, (8, 128), 1)
    copies = []
    for n, (out, factors) in enumerate(((update, z), (last, w))):
        ends = factors[0] * edges[0]
        for a in range(1, len(factors)):
            ends = ends + factors[a] * edges[a]
        for g, planes in enumerate((slice(0, 8), slice(8, 16), slice(16, 22))):
            count = planes.stop - planes.start
            for r in range(8):
                row = factors[0] * own[r, planes, :]
                for a in range(1, len(factors)):
                    part = inner if is_inner(a, r + DEPTH) else outer
                    row = row + factors[a] * part[a - 1, r, planes, :]
                at = PITCH * (r + DEPTH)
                left = pltpu.roll(ends[planes], (EDGE - at - 3) % EDGE, 1)[:, 0:128]
                right = pltpu.roll(ends[planes], (253 - at - 12) % EDGE, 1)[:, 128:256]
                inside = lane[0:count]
                parts[n, planes, r, 0:128] = jnp.where(inside < DEPTH, left, row[:, 0:128])
                parts[n, planes, r, 128:384] = row[:, 128:384]
                parts[n, planes, r, 384:512] = jnp.where(
                    inside >= 128 - DEPTH, right, row[:, 384:512]
                )
            copies.append(
                pltpu.make_async_copy(parts.at[n, planes], out.at[planes], sems.at[3 * n + g])
            )
            copies[-1].start()
    for copy in copies:
        copy.wait()


def call(kernel, outs, scratch=(), flops=0, bytes_accessed=0, limit=8, in_hbm=0, out_hbm=0):
    single = not isinstance(outs, (list, tuple))
    extra = {"in_specs": [pl.BlockSpec(memory_space=pltpu.HBM)] * in_hbm} if in_hbm else {}
    if out_hbm:
        extra["out_specs"] = (pl.BlockSpec(memory_space=pltpu.HBM),) * out_hbm
    return pl.pallas_call(
        kernel,
        out_shape=outs if single else tuple(outs),
        scratch_shapes=list(scratch),
        **extra,
        compiler_params=pltpu.CompilerParams(vmem_limit_bytes=limit * 1024 * 1024),
        cost_estimate=pl.CostEstimate(
            flops=flops, bytes_accessed=bytes_accessed, transcendentals=0
        ),
    )


def f32(*shape):
    return jax.ShapeDtypeStruct(shape, jnp.float32)


def swapped(shard, axis, start):
    pairs = []
    for i in range(start, lax.axis_size(axis) - 1, 2):
        pairs += [(i, i + 1), (i + 1, i)]
    return lax.ppermute(shard, axis, pairs)


def body(rhs, viscosity, cell_mask, friction, stiffness):
    devices = lax.axis_size("rx") * lax.axis_size("ry")
    natural = [
        pltpu.with_memory_space_constraint(x, pltpu.HBM)
        for x in (rhs.reshape(22, 8, 512), viscosity, cell_mask, friction, stiffness.transpose(1, 0, 2))
    ]
    first, second, *local, stiff = call(
        rows_kernel,
        (f32(DEPTH, 48, 512), f32(DEPTH, 48, 512), f32(22, 8, 512), f32(10, 2, 8, 512),
         jax.ShapeDtypeStruct((8, 512), jnp.int32), f32(8, 512), f32(12, 2, 12)),
        [pltpu.VMEM((2, 48, 512), jnp.float32), pltpu.SemaphoreType.DMA((5,))],
        bytes_accessed=10**6,
        in_hbm=5,
    )(*natural)
    first_rows = swapped(first, "rx", 0)
    second_rows = swapped(second, "rx", 1)
    own, packs, weights, *prepared = call(
        own_kernel,
        (
            f32(8, 48, LANES),
            f32(48, EDGE),
            jax.ShapeDtypeStruct((2, GROUPS, 3 * HALF), jnp.bfloat16),
            f32(8, 96, LANES),
            f32(8, 24, LANES),
            f32(3, 8, 24, LANES),
            jax.ShapeDtypeStruct((3, 2, BLOCK, LANES), jnp.bfloat16),
            f32(3, 24, LANES),
            f32(3, 2, 24, LANES),
        ),
        [pltpu.VMEM((2, 8 * BLOCK, LANES), jnp.bfloat16)],
        flops=10**9,
        bytes_accessed=10**6,
        limit=16,
    )(*local, stiff)
    inner = prepared[2]
    packs = call(cols_kernel, f32(48, EDGE), bytes_accessed=10**6)(packs, first_rows, second_rows)
    first_cols = swapped(packs, "ry", 0)
    second_cols = swapped(packs, "ry", 1)
    outer, line = call(
        main_kernel,
        (f32(3, 8, 24, LANES), f32(8, 128)),
        [
            pltpu.VMEM((NROW - 1, 96, LANES), jnp.float32),
            pltpu.VMEM((NROW, 24, LANES), jnp.float32),
            pltpu.VMEM((4, NROW, 24, LANES), jnp.float32),
            pltpu.VMEM((2, NROW * BLOCK, LANES), jnp.bfloat16),
        ],
        flops=2 * 10**9,
        bytes_accessed=3 * 10**6,
        limit=24,
    )(own, weights, *prepared, first_rows, second_rows, stiff)
    edges, gram = call(
        edge_kernel,
        (f32(4, 24, EDGE), f32(devices, 128)),
        [pltpu.VMEM((96, EDGE), jnp.float32)],
        flops=10**8,
        bytes_accessed=10**6,
    )(packs, first_cols, second_cols, stiff, weights, line)
    grams = lax.all_to_all(gram.reshape(devices, 1, 128), ("rx", "ry"), 0, 0)
    update, last = call(
        combine_kernel,
        (f32(22, 8, 512),) * 2,
        [pltpu.VMEM((2, 22, 8, 512), jnp.float32), pltpu.SemaphoreType.DMA((6,))],
        bytes_accessed=3 * 10**6,
        out_hbm=2,
    )(
        own, inner, outer, edges, grams.reshape(devices, 128), stiff
    )
    return update.reshape(2, 11, 8, 512), last.reshape(2, 11, 8, 512)


def solution(mesh):
    in_specs = (
        P(None, None, "rx", "ry"),
        P(None, None, "rx", "ry"),
        P("rx", "ry"),
        P("rx", "ry"),
        P(),
    )
    out_specs = (P(None, None, "rx", "ry"), P(None, None, "rx", "ry"))
    return jax.shard_map(body, mesh=mesh, in_specs=in_specs, out_specs=out_specs, check_vma=False)
```

```python
import jax
import jax.numpy as jnp
from jax import lax
from jax.experimental import pallas as pl
from jax.experimental.pallas import tpu as pltpu
from jax.sharding import PartitionSpec as P


DEPTH = 3
NROW = 8 + 2 * DEPTH
LANES = 512
PITCH = 18
EDGE = 256
PAIRS = [(a, b) for a in range(4) for b in range(a, 4)]
HALF = 80
BLOCK = 2 * HALF
GROUPS = 144


def shift_of(stiff):
    rows = lax.broadcasted_iota(jnp.int32, (12, 12), 0)
    cols = lax.broadcasted_iota(jnp.int32, (12, 12), 1)
    trace = jnp.sum(jnp.where(rows == cols, stiff[:, 0, :] + stiff[:, 1, :], 0.0))
    return 1.0 + trace * (1.2 * 10.0 / 22.0)


def own_row(out, rhs, visc, mask, fric, row):
    ice = mask[row : row + 1, :].astype(jnp.float32)
    out[0:22, 0:512] = rhs[:, row, :]
    out[22:23, 0:512] = jnp.ones_like(ice)
    out[23:24, 0:512] = fric[row : row + 1, :]
    out[24:34, 0:512] = visc[:, 0, row, :] * ice
    out[34:44, 0:512] = visc[:, 1, row, :] * ice
    out[44:48, 0:512] = jnp.zeros((4, 512), jnp.float32)


def odd_along(axis):
    return lax.rem(lax.axis_index(axis), 2) == 1


def rows_kernel(
    rhs, visc, mask, fric, stiff,
    first, second, rhs_out, visc_out, mask_out, fric_out, stiff_out,
    work, sems,
):
    sources = (rhs, visc, mask, fric, stiff)
    targets = (rhs_out, visc_out, mask_out, fric_out, stiff_out)
    copies = [
        pltpu.make_async_copy(src, dst, sems.at[n])
        for n, (src, dst) in enumerate(zip(sources, targets))
    ]
    for copy in copies:
        copy.start()
    for copy in copies:
        copy.wait()
    odd = odd_along("rx")
    for j in range(DEPTH):
        own_row(work.at[0], rhs_out, visc_out, mask_out, fric_out, 8 - DEPTH + j)
        own_row(work.at[1], rhs_out, visc_out, mask_out, fric_out, j)
        up, down = (work[0], work[1])
        first[j] = jnp.where(odd, down, up)
        second[j] = jnp.where(odd, up, down)


def pack_row(row, i, lane, packed):
    ends = jnp.concatenate([row[:, 0:128], row[:, 384:512]], axis=1)
    at = lane - PITCH * i
    packed = jnp.where((at >= 0) & (at < 9), pltpu.roll(ends, (PITCH * i + 3) % EDGE, 1), packed)
    return jnp.where((at >= 9) & (at < 18), pltpu.roll(ends, (PITCH * i + 15) % EDGE, 1), packed)


def cols_kernel(packs, second_rows, first_rows, out):
    odd_row = odd_along("rx")
    lane = lax.broadcasted_iota(jnp.int32, (48, 128), 1)
    halves = [packs[:, 0:128], packs[:, 128:256]]
    for j in range(DEPTH):
        one, two = [
            jnp.where(lane < 64, rows[j, :, 0:128], rows[j, :, 384:512])
            for rows in (first_rows, second_rows)
        ]
        low, high = (jnp.where(odd_row, one, two), jnp.where(odd_row, two, one))
        for half, row, i in ((0, low, j), (1, high, j + 8 + DEPTH)):
            start = PITCH * i - 128 * half
            at = lane - start
            packed = jnp.where((at >= 0) & (at < 9), pltpu.roll(row, start + 3, 1), halves[half])
            halves[half] = jnp.where(
                (at >= 9) & (at < 18), pltpu.roll(row, (start + 15) % 128, 1), packed
            )
    out[:, 0:128] = halves[0]
    out[:, 128:256] = halves[1]


def weights_kernel(stiff, weights):
    row = lax.broadcasted_iota(jnp.int32, (GROUPS, 12), 0)
    col = lax.broadcasted_iota(jnp.int32, (GROUPS, 12), 1)

    def of_row(r):
        group, plane = (r // 24, r % 24)
        slot, lev = (group // 2, group % 2)
        comp, level = (plane // 11, plane % 11)
        layer = level - lev
        good = (plane < 22) & (layer >= 0) & (layer < 10)
        return comp * 6 + lev * 3 + slot, layer, good

    pick = jnp.where(of_row(row)[0] == col, 1.0, 0.0)
    r = lax.broadcasted_iota(jnp.int32, (GROUPS, 3 * HALF), 0)
    k = lax.broadcasted_iota(jnp.int32, (GROUPS, 3 * HALF), 1)
    _, layer, good = of_row(r)
    part = (k % HALF) // 24
    plane = (k % HALF) % 24
    lev_in = plane % 11 - layer
    good = good & (part < 3) & (plane < 22)
    q = lax.broadcasted_iota(jnp.int32, (12, 3 * HALF), 0)
    kq = lax.broadcasted_iota(jnp.int32, (12, 3 * HALF), 1)
    comp_in = ((kq % HALF) % 24) // 11
    block = kq // HALF
    for tri in range(2):
        first, second, third = ((0, 2, 1), (2, 0, 1))[tri]
        place = jnp.where(block == 0, first, jnp.where(block == 1, second, third))
        rows = jnp.dot(
            pick, stiff[:, tri, :], precision=lax.Precision.HIGHEST, preferred_element_type=jnp.float32
        )
        total = jnp.zeros((GROUPS, 3 * HALF), jnp.float32)
        for lev in range(2):
            sel = jnp.where(comp_in * 6 + lev * 3 + place == q, 1.0, 0.0)
            spread = jnp.dot(
                rows, sel, precision=lax.Precision.HIGHEST, preferred_element_type=jnp.float32
            )
            total = jnp.where(good & (lev_in == lev), spread, total)
        high = total.astype(jnp.bfloat16).astype(jnp.float32)
        weights[tri] = jnp.where(part == 2, total - high, high).astype(jnp.bfloat16)


def split_rows(x):
    high = x.astype(jnp.bfloat16).astype(jnp.float32)
    pad = jnp.zeros((HALF - 72, x.shape[1]), jnp.float32)
    return jnp.concatenate([high, x - high, high, pad], axis=0).astype(jnp.bfloat16)


def put_operand(operand, i, x):
    operand[i * BLOCK : i * BLOCK + HALF, :] = split_rows(x)
    operand[i * BLOCK + HALF : (i + 1) * BLOCK, :] = split_rows(pltpu.roll(x, LANES - 1, 1))


def put_scale(out, coefs):
    zeros = jnp.zeros((24, out.shape[1]), jnp.float32)
    for tri in range(2):
        for lev in range(2):
            base = 48 * tri + 24 * lev
            out[base : base + 24, :] = zeros
            out[base + lev : base + lev + 10, :] = coefs[tri]
            out[base + 11 + lev : base + 21 + lev, :] = coefs[tri]


def grown_of(scale, mixed):
    parts = []
    for tri in range(2):
        upper = scale[48 * tri : 48 * tri + 24, :]
        lower = scale[48 * tri + 24 : 48 * tri + 48, :]
        for slot in range(3):
            at = 48 * slot
            parts.append(upper * mixed[tri][at : at + 24] + lower * mixed[tri][at + 24 : at + 48])
    return parts[0], parts[1] + parts[3], parts[2] + parts[5], parts[4]


def inner_products(vectors, sums, lanes):
    result = []
    for total, (a, b) in zip(sums, PAIRS):
        product = vectors[a] * vectors[b]
        for s in range(0, 24, 8):
            for l in range(0, lanes, 128):
                total = total + product[s : s + 8, l : l + 128]
        result.append(total)
    return tuple(result)


def line_of(sums):
    rows = [jnp.sum(total, axis=0, keepdims=True) for total in sums]
    rows.append(jnp.zeros((16 - len(rows), 128), jnp.float32))
    totals = jnp.sum(jnp.concatenate(rows, axis=0), axis=1, keepdims=True)
    row = lax.broadcasted_iota(jnp.int32, (16, 128), 0)
    place = lax.broadcasted_iota(jnp.int32, (16, 128), 1)
    line = jnp.sum(jnp.where(place == row, totals, 0.0), axis=0, keepdims=True)
    return jnp.broadcast_to(line, (8, 128))


def no_sums():
    return tuple(jnp.zeros((8, 128), jnp.float32) for _ in PAIRS)


def products(weights, source, i):
    start = i * BLOCK
    return [
        jnp.dot(
            weights[tri],
            source[start + HALF * tri : start + HALF * (tri + 3), :],
            preferred_element_type=jnp.float32,
        )
        for tri in range(2)
    ]


def bottom_planes(lanes):
    plane = lax.broadcasted_iota(jnp.int32, (24, lanes), 0)
    return (plane == 0) | (plane == 11)


def field_planes(row):
    plane = lax.broadcasted_iota(jnp.int32, (24, row.shape[1]), 0)
    return jnp.where(plane < 22, row[0:24, :], 0.0)


def diag_planes(row, theta):
    on_bottom = jnp.where(bottom_planes(row.shape[1]), row[23:24, :], 0.0)
    return row[22:23, :] * (1.0 - theta) + on_bottom


def is_inner(k, i):
    return DEPTH + k <= i <= DEPTH + 7 - k


def own_kernel(
    rhs, visc, mask, fric, stiff,
    own, packs, weights, scale, diag, powers, bounds, low_parts, high_parts,
    operand,
):
    weights_kernel(stiff, weights)
    theta = shift_of(stiff)
    lane = lax.broadcasted_iota(jnp.int32, (48, EDGE), 1)
    packed = jnp.zeros((48, EDGE), jnp.float32)
    for r in range(8):
        own_row(own.at[r], rhs, visc, mask, fric, r)
        row = own[r]
        packed = pack_row(row, r + DEPTH, lane, packed)
        put_operand(operand.at[0], r, field_planes(row))
        diag[r] = diag_planes(row, theta)
        put_scale(scale.at[r], (row[24:34, :], row[34:44, :]))
    packs[...] = packed
    for step in range(1, DEPTH + 1):
        source = operand.at[(step - 1) % 2]
        target = operand.at[step % 2]
        first, last = (step - 1, 8 - step)
        bounds[step - 1, 0] = source[first * BLOCK : (first + 1) * BLOCK, :]
        bounds[step - 1, 1] = source[last * BLOCK : (last + 1) * BLOCK, :]
        for r in range(first, last):
            a, b, c, d = grown_of(scale[r], products(weights, source, r))
            if r == first:
                low_parts[step - 1] = a + pltpu.roll(c, 1, 1)
            else:
                total = a + upper + pltpu.roll(c + across, 1, 1)
                before = powers[step - 2, r] if step > 1 else field_planes(own[r])
                x = total + diag[r] * before
                powers[step - 1, r] = x
                if step < DEPTH:
                    put_operand(target, r, x)
            upper, across = (b, d)
        high_parts[step - 1, 0] = upper
        high_parts[step - 1, 1] = across


def main_kernel(
    own, weights, own_scale, own_diag, inner, bounds, low_parts, high_parts, second_rows, first_rows, stiff,
    outer, line,
    scale, diag, field, operand,
):
    odd_row = odd_along("rx")
    theta = shift_of(stiff)
    real = {}
    for i in (0, 1, 2, 11, 12, 13):
        if i < DEPTH:
            row = jnp.where(odd_row, first_rows[i], second_rows[i])
        else:
            j = i - 8 - DEPTH
            row = jnp.where(odd_row, second_rows[j], first_rows[j])
            real[i] = row[22:23, :]
        x = field_planes(row)
        field[0, i] = x
        put_operand(operand.at[0], i, x)
        diag[i] = diag_planes(row, theta)
        if i < NROW - 1:
            put_scale(scale.at[i], (row[24:34, :], row[34:44, :]))

    def power(k, i):
        if k == 0 and is_inner(0, i):
            return field_planes(own[i - DEPTH])
        return inner[k - 1, i - DEPTH] if is_inner(k, i) else field[k, i]

    for step in range(1, DEPTH + 1):
        source = operand.at[(step - 1) % 2]
        target = operand.at[step % 2]
        for side, i in ((0, DEPTH + step - 1), (1, DEPTH + 8 - step)):
            source[i * BLOCK : (i + 1) * BLOCK, :] = bounds[step - 1, side]

        def grown(i, source=source):
            is_own = is_inner(0, i)
            return grown_of(own_scale[i - DEPTH] if is_own else scale[i], products(weights, source, i))

        def put(i, total, step=step, target=target):
            if i in real:
                total = total * real[i]
            x = total + (own_diag[i - DEPTH] if is_inner(0, i) else diag[i]) * power(step - 1, i)
            field[step, i] = x
            if is_inner(0, i):
                outer[step - 1, i - DEPTH] = x
            if step < DEPTH:
                put_operand(target, i, x)

        first = step - 1
        _, upper, _, across = grown(first)
        for i in range(first + 1, first + 3):
            a, b, c, d = grown(i)
            put(i, a + upper + pltpu.roll(c + across, 1, 1))
            upper, across = (b, d)
        put(first + 3, low_parts[step - 1] + upper + pltpu.roll(across, 1, 1))
        upper, across = (high_parts[step - 1, 0], high_parts[step - 1, 1])
        for i in range(11 - step, 14 - step):
            a, b, c, d = grown(i)
            put(i, a + upper + pltpu.roll(c + across, 1, 1))
            upper, across = (b, d)

    lane = lax.broadcasted_iota(jnp.int32, (24, LANES), 1)
    inside = (lane >= DEPTH) & (lane < LANES - DEPTH)
    sums = no_sums()
    for r in range(8):
        vectors = [jnp.where(inside, power(a, r + DEPTH), 0.0) for a in range(4)]
        sums = inner_products(vectors, sums, LANES)
    line[...] = line_of(sums)


def edge_kernel(packs, first_cols, second_cols, stiff, weights, line, edges, gram, scale):
    odd_col = odd_along("ry")
    theta = shift_of(stiff)
    at = lax.rem(lax.broadcasted_iota(jnp.int32, (48, EDGE), 1), PITCH)
    from_left = jnp.where(odd_col, first_cols[...], second_cols[...])
    from_right = jnp.where(odd_col, second_cols[...], first_cols[...])
    full = jnp.where(at < 3, from_left, jnp.where(at >= 15, from_right, packs[...]))
    put_scale(scale, (full[24:34], full[34:44]))
    real = full[22:23]
    diag = diag_planes(full, theta)
    x = field_planes(full)
    vectors = [x]
    for _ in range(DEPTH):
        corners = [
            split_rows(pltpu.roll(x, (EDGE - by) % EDGE, 1) if by else x)
            for by in (0, 1, PITCH, PITCH + 1)
        ]
        mixed = [
            jnp.dot(
                weights[tri],
                jnp.concatenate(corners[tri : tri + 3], axis=0),
                preferred_element_type=jnp.float32,
            )
            for tri in range(2)
        ]
        a, b, c, d = grown_of(scale[...], mixed)
        total = a + pltpu.roll(b, PITCH, 1) + pltpu.roll(c + pltpu.roll(d, PITCH, 1), 1, 1)
        x = real * total + diag * x
        vectors.append(x)
    for a in range(4):
        edges[a] = vectors[a]
    lane = lax.broadcasted_iota(jnp.int32, (24, EDGE), 1)
    at = lax.rem(lane, PITCH)
    mine = (lane >= PITCH * DEPTH) & (lane < PITCH * (DEPTH + 8))
    mine = mine & (((at >= 3) & (at < 6)) | ((at >= 12) & (at < 15)))
    sums = inner_products([jnp.where(mine, v, 0.0) for v in vectors], no_sums(), EDGE)
    total = line[...] + line_of(sums)
    gram[...] = jnp.broadcast_to(total[0:1], gram.shape)


def combine_kernel(own, inner, outer, edges, grams, stiff, update, last, parts, sems):
    theta = shift_of(stiff)
    entry = jnp.sum(grams[...], axis=0, keepdims=True)
    place = lax.broadcasted_iota(jnp.int32, (1, 128), 1)
    g = {}
    for n, pair in enumerate(PAIRS):
        g[pair] = jnp.sum(jnp.where(place == n, entry, 0.0), axis=1, keepdims=True)
    upper = [[None] * 4 for _ in range(4)]
    inverse = [None] * 4
    for a in range(4):
        for b in range(a, 4):
            value = g[a, b]
            for c in range(a):
                value = value - upper[c][a] * upper[c][b]
            if a == b:
                inverse[a] = lax.rsqrt(value)
                upper[a][a] = value * inverse[a]
            else:
                upper[a][b] = value * inverse[a]
    zero = jnp.zeros((1, 1), jnp.float32)
    table = [
        [
            (upper[a][b + 1] if a <= b + 1 else zero) + (theta * upper[a][b] if a <= b else zero)
            for b in range(3)
        ]
        for a in range(4)
    ]
    target = [upper[0][0], zero, zero, zero]
    turned = [None] * 3
    for col in range(3):
        first, second = (table[col][col], table[col + 1][col])
        turned[col] = lax.rsqrt(first * first + second * second)
        cosine, sine = (first * turned[col], second * turned[col])
        for c in range(col, 3):
            one, two = (table[col][c], table[col + 1][c])
            table[col][c] = cosine * one + sine * two
            table[col + 1][c] = cosine * two - sine * one
        one, two = (target[col], target[col + 1])
        target[col] = cosine * one + sine * two
        target[col + 1] = cosine * two - sine * one
    z = [None] * 3
    for col in (2, 1, 0):
        value = target[col]
        for c in range(col + 1, 3):
            value = value - table[col][c] * z[c]
        z[col] = value * turned[col]
    w = [None] * 4
    w[3] = inverse[3]
    for a in (2, 1, 0):
        value = zero
        for c in range(a + 1, 4):
            value = value - upper[a][c] * w[c]
        w[a] = value * inverse[a]
    lane = lax.broadcasted_iota(jnp.int32, (8, 128), 1)
    copies = []
    for n, (out, factors) in enumerate(((update, z), (last, w))):
        ends = factors[0] * edges[0]
        for a in range(1, len(factors)):
            ends = ends + factors[a] * edges[a]
        for g, planes in enumerate((slice(0, 8), slice(8, 16), slice(16, 22))):
            count = planes.stop - planes.start
            for r in range(8):
                row = factors[0] * own[r, planes, :]
                for a in range(1, len(factors)):
                    part = inner if is_inner(a, r + DEPTH) else outer
                    row = row + factors[a] * part[a - 1, r, planes, :]
                at = PITCH * (r + DEPTH)
                left = pltpu.roll(ends[planes], (EDGE - at - 3) % EDGE, 1)[:, 0:128]
                right = pltpu.roll(ends[planes], (253 - at - 12) % EDGE, 1)[:, 128:256]
                inside = lane[0:count]
                parts[n, planes, r, 0:128] = jnp.where(inside < DEPTH, left, row[:, 0:128])
                parts[n, planes, r, 128:384] = row[:, 128:384]
                parts[n, planes, r, 384:512] = jnp.where(
                    inside >= 128 - DEPTH, right, row[:, 384:512]
                )
            copies.append(
                pltpu.make_async_copy(parts.at[n, planes], out.at[planes], sems.at[3 * n + g])
            )
            copies[-1].start()
    for copy in copies:
        copy.wait()


def call(kernel, outs, scratch=(), flops=0, bytes_accessed=0, limit=8, in_hbm=0, out_hbm=0):
    single = not isinstance(outs, (list, tuple))
    extra = {"in_specs": [pl.BlockSpec(memory_space=pltpu.HBM)] * in_hbm} if in_hbm else {}
    if out_hbm:
        extra["out_specs"] = (pl.BlockSpec(memory_space=pltpu.HBM),) * out_hbm
    return pl.pallas_call(
        kernel,
        out_shape=outs if single else tuple(outs),
        scratch_shapes=list(scratch),
        **extra,
        compiler_params=pltpu.CompilerParams(vmem_limit_bytes=limit * 1024 * 1024),
        cost_estimate=pl.CostEstimate(
            flops=flops, bytes_accessed=bytes_accessed, transcendentals=0
        ),
    )


def f32(*shape):
    return jax.ShapeDtypeStruct(shape, jnp.float32)


def swapped(shard, axis, start):
    pairs = []
    for i in range(start, lax.axis_size(axis) - 1, 2):
        pairs += [(i, i + 1), (i + 1, i)]
    return lax.ppermute(shard, axis, pairs)


def body(rhs, viscosity, cell_mask, friction, stiffness):
    devices = lax.axis_size("rx") * lax.axis_size("ry")
    natural = [
        pltpu.with_memory_space_constraint(x, pltpu.HBM)
        for x in (rhs.reshape(22, 8, 512), viscosity, cell_mask, friction, stiffness.transpose(1, 0, 2))
    ]
    first, second, *local, stiff = call(
        rows_kernel,
        (f32(DEPTH, 48, 512), f32(DEPTH, 48, 512), f32(22, 8, 512), f32(10, 2, 8, 512),
         jax.ShapeDtypeStruct((8, 512), jnp.int32), f32(8, 512), f32(12, 2, 12)),
        [pltpu.VMEM((2, 48, 512), jnp.float32), pltpu.SemaphoreType.DMA((5,))],
        bytes_accessed=10**6,
        in_hbm=5,
    )(*natural)
    first_rows = swapped(first, "rx", 0)
    second_rows = swapped(second, "rx", 1)
    own, packs, weights, *prepared = call(
        own_kernel,
        (
            f32(8, 48, LANES),
            f32(48, EDGE),
            jax.ShapeDtypeStruct((2, GROUPS, 3 * HALF), jnp.bfloat16),
            f32(8, 96, LANES),
            f32(8, 24, LANES),
            f32(3, 8, 24, LANES),
            jax.ShapeDtypeStruct((3, 2, BLOCK, LANES), jnp.bfloat16),
            f32(3, 24, LANES),
            f32(3, 2, 24, LANES),
        ),
        [pltpu.VMEM((2, 8 * BLOCK, LANES), jnp.bfloat16)],
        flops=10**9,
        bytes_accessed=10**6,
        limit=16,
    )(*local, stiff)
    inner = prepared[2]
    packs = call(cols_kernel, f32(48, EDGE), bytes_accessed=10**6)(packs, second_rows, first_rows)
    first_cols = swapped(packs, "ry", 0)
    second_cols = swapped(packs, "ry", 1)
    outer, line = call(
        main_kernel,
        (f32(3, 8, 24, LANES), f32(8, 128)),
        [
            pltpu.VMEM((NROW - 1, 96, LANES), jnp.float32),
            pltpu.VMEM((NROW, 24, LANES), jnp.float32),
            pltpu.VMEM((4, NROW, 24, LANES), jnp.float32),
            pltpu.VMEM((2, NROW * BLOCK, LANES), jnp.bfloat16),
        ],
        flops=2 * 10**9,
        bytes_accessed=3 * 10**6,
        limit=24,
    )(own, weights, *prepared, second_rows, first_rows, stiff)
    edges, gram = call(
        edge_kernel,
        (f32(4, 24, EDGE), f32(devices, 128)),
        [pltpu.VMEM((96, EDGE), jnp.float32)],
        flops=10**8,
        bytes_accessed=10**6,
    )(packs, first_cols, second_cols, stiff, weights, line)
    grams = lax.all_to_all(gram.reshape(devices, 1, 128), ("rx", "ry"), 0, 0)
    update, last = call(
        combine_kernel,
        (f32(22, 8, 512),) * 2,
        [pltpu.VMEM((2, 22, 8, 512), jnp.float32), pltpu.SemaphoreType.DMA((6,))],
        bytes_accessed=3 * 10**6,
        out_hbm=2,
    )(
        own, inner, outer, edges, grams.reshape(devices, 128), stiff
    )
    return update.reshape(2, 11, 8, 512), last.reshape(2, 11, 8, 512)


def solution(mesh):
    in_specs = (
        P(None, None, "rx", "ry"),
        P(None, None, "rx", "ry"),
        P("rx", "ry"),
        P("rx", "ry"),
        P(),
    )
    out_specs = (P(None, None, "rx", "ry"), P(None, None, "rx", "ry"))
    return jax.shard_map(body, mesh=mesh, in_specs=in_specs, out_specs=out_specs, check_vma=False)
```

```python
import jax
import jax.numpy as jnp
from jax import lax
from jax.experimental import pallas as pl
from jax.experimental.pallas import tpu as pltpu
from jax.sharding import PartitionSpec as P


DEPTH = 3
NROW = 8 + 2 * DEPTH
LANES = 512
PITCH = 18
EDGE = 256
PAIRS = [(a, b) for a in range(4) for b in range(a, 4)]
HALF = 80
BLOCK = 2 * HALF
GROUPS = 144


def shift_of(stiff):
    rows = lax.broadcasted_iota(jnp.int32, (12, 12), 0)
    cols = lax.broadcasted_iota(jnp.int32, (12, 12), 1)
    trace = jnp.sum(jnp.where(rows == cols, stiff[:, 0, :] + stiff[:, 1, :], 0.0))
    return 1.0 + trace * (1.2 * 10.0 / 22.0)


def own_row(out, rhs, visc, mask, fric, row):
    ice = mask[row : row + 1, :].astype(jnp.float32)
    out[0:22, 0:512] = rhs[:, row, :]
    out[22:23, 0:512] = jnp.ones_like(ice)
    out[23:24, 0:512] = fric[row : row + 1, :]
    out[24:34, 0:512] = visc[:, 0, row, :] * ice
    out[34:44, 0:512] = visc[:, 1, row, :] * ice
    out[44:48, 0:512] = jnp.zeros((4, 512), jnp.float32)


def odd_along(axis):
    return lax.rem(lax.axis_index(axis), 2) == 1


def rows_kernel(
    rhs, visc, mask, fric, stiff,
    first, second, rhs_out, visc_out, mask_out, fric_out, stiff_out,
    work, sems,
):
    sources = (rhs, visc, mask, fric, stiff)
    targets = (rhs_out, visc_out, mask_out, fric_out, stiff_out)
    copies = [
        pltpu.make_async_copy(src, dst, sems.at[n])
        for n, (src, dst) in enumerate(zip(sources, targets))
    ]
    for copy in copies:
        copy.start()
    for copy in copies:
        copy.wait()
    odd = odd_along("rx")
    for j in range(DEPTH):
        own_row(work.at[0], rhs_out, visc_out, mask_out, fric_out, 8 - DEPTH + j)
        own_row(work.at[1], rhs_out, visc_out, mask_out, fric_out, j)
        up, down = (work[0], work[1])
        first[j] = jnp.where(odd, down, up)
        second[j] = jnp.where(odd, up, down)


def pack_row(row, i, lane, packed):
    ends = jnp.concatenate([row[:, 0:128], row[:, 384:512]], axis=1)
    at = lane - PITCH * i
    packed = jnp.where((at >= 0) & (at < 9), pltpu.roll(ends, (PITCH * i + 3) % EDGE, 1), packed)
    return jnp.where((at >= 9) & (at < 18), pltpu.roll(ends, (PITCH * i + 15) % EDGE, 1), packed)


def cols_kernel(packs, second_rows, first_rows, out):
    odd_row = odd_along("rx")
    lane = lax.broadcasted_iota(jnp.int32, (48, 128), 1)
    halves = [packs[:, 0:128], packs[:, 128:256]]
    for j in range(DEPTH):
        one, two = [
            jnp.where(lane < 64, rows[j, :, 0:128], rows[j, :, 384:512])
            for rows in (first_rows, second_rows)
        ]
        low, high = (jnp.where(odd_row, one, two), jnp.where(odd_row, two, one))
        for half, row, i in ((0, low, j), (1, high, j + 8 + DEPTH)):
            start = PITCH * i - 128 * half
            at = lane - start
            packed = jnp.where((at >= 0) & (at < 9), pltpu.roll(row, start + 3, 1), halves[half])
            halves[half] = jnp.where(
                (at >= 9) & (at < 18), pltpu.roll(row, (start + 15) % 128, 1), packed
            )
    out[:, 0:128] = halves[0]
    out[:, 128:256] = halves[1]


def weights_kernel(stiff, weights):
    row = lax.broadcasted_iota(jnp.int32, (GROUPS, 12), 0)
    col = lax.broadcasted_iota(jnp.int32, (GROUPS, 12), 1)

    def of_row(r):
        group, plane = (r // 24, r % 24)
        slot, lev = (group // 2, group % 2)
        comp, level = (plane // 11, plane % 11)
        layer = level - lev
        good = (plane < 22) & (layer >= 0) & (layer < 10)
        return comp * 6 + lev * 3 + slot, layer, good

    pick = jnp.where(of_row(row)[0] == col, 1.0, 0.0)
    r = lax.broadcasted_iota(jnp.int32, (GROUPS, 3 * HALF), 0)
    k = lax.broadcasted_iota(jnp.int32, (GROUPS, 3 * HALF), 1)
    _, layer, good = of_row(r)
    part = (k % HALF) // 24
    plane = (k % HALF) % 24
    lev_in = plane % 11 - layer
    good = good & (part < 3) & (plane < 22)
    q = lax.broadcasted_iota(jnp.int32, (12, 3 * HALF), 0)
    kq = lax.broadcasted_iota(jnp.int32, (12, 3 * HALF), 1)
    comp_in = ((kq % HALF) % 24) // 11
    block = kq // HALF
    for tri in range(2):
        first, second, third = ((0, 2, 1), (2, 0, 1))[tri]
        place = jnp.where(block == 0, first, jnp.where(block == 1, second, third))
        rows = jnp.dot(
            pick, stiff[:, tri, :], precision=lax.Precision.HIGHEST, preferred_element_type=jnp.float32
        )
        total = jnp.zeros((GROUPS, 3 * HALF), jnp.float32)
        for lev in range(2):
            sel = jnp.where(comp_in * 6 + lev * 3 + place == q, 1.0, 0.0)
            spread = jnp.dot(
                rows, sel, precision=lax.Precision.HIGHEST, preferred_element_type=jnp.float32
            )
            total = jnp.where(good & (lev_in == lev), spread, total)
        high = total.astype(jnp.bfloat16).astype(jnp.float32)
        weights[tri] = jnp.where(part == 2, total - high, high).astype(jnp.bfloat16)


def split_rows(x):
    high = x.astype(jnp.bfloat16).astype(jnp.float32)
    pad = jnp.zeros((HALF - 72, x.shape[1]), jnp.float32)
    return jnp.concatenate([high, x - high, high, pad], axis=0).astype(jnp.bfloat16)


def put_operand(operand, i, x):
    operand[i * BLOCK : i * BLOCK + HALF, :] = split_rows(x)
    operand[i * BLOCK + HALF : (i + 1) * BLOCK, :] = split_rows(pltpu.roll(x, LANES - 1, 1))


def put_scale(out, coefs):
    zeros = jnp.zeros((24, out.shape[1]), jnp.float32)
    for tri in range(2):
        for lev in range(2):
            base = 48 * tri + 24 * lev
            out[base : base + 24, :] = zeros
            out[base + lev : base + lev + 10, :] = coefs[tri]
            out[base + 11 + lev : base + 21 + lev, :] = coefs[tri]


def grown_of(scale, mixed):
    parts = []
    for tri in range(2):
        upper = scale[48 * tri : 48 * tri + 24, :]
        lower = scale[48 * tri + 24 : 48 * tri + 48, :]
        for slot in range(3):
            at = 48 * slot
            parts.append(upper * mixed[tri][at : at + 24] + lower * mixed[tri][at + 24 : at + 48])
    return parts[0], parts[1] + parts[3], parts[2] + parts[5], parts[4]


def inner_products(vectors, sums, lanes):
    result = []
    for (high, low), (a, b) in zip(sums, PAIRS):
        product = vectors[a] * vectors[b]
        terms = [
            product[s : s + 8, l : l + 128] for s in range(0, 24, 8) for l in range(0, lanes, 128)
        ]
        while len(terms) > 1:
            terms = [sum(terms[n : n + 2][1:], terms[n]) for n in range(0, len(terms), 2)]
        high, rest = two_sum(high, terms[0])
        result.append((high, low + rest))
    return tuple(result)


def two_sum(a, b):
    total = a + b
    back = total - a
    return total, (a - (total - back)) + (b - back)


def pair_of(high, low):
    total = high + low
    return total, low - (total - high)


def parts_of(a):
    wide = a * 4097.0
    high = wide - (wide - a)
    return high, a - high


def pair_times(x, y):
    product = x[0] * y[0]
    (xh, xl), (yh, yl) = (parts_of(x[0]), parts_of(y[0]))
    rest = ((xh * yh - product) + xh * yl + xl * yh) + xl * yl
    return pair_of(product, rest + (x[0] * y[1] + x[1] * y[0]))


def pair_less(x, y):
    total, rest = two_sum(x[0], -y[0])
    return pair_of(total, rest + (x[1] - y[1]))


def pair_over(x, y):
    zero = jnp.zeros_like(x[0])
    first = x[0] / y[0]
    rest = pair_less(x, pair_times(y, (first, zero)))
    return pair_of(first, rest[0] / y[0])


def folded(high, low, axis, shifts):
    for by in shifts:
        total, rest = two_sum(high, pltpu.roll(high, by, axis))
        low = low + pltpu.roll(low, by, axis) + rest
        high = total
    return high, low


def line_of(sums):
    rows = [folded(high, low, 0, (4, 2, 1)) for high, low in sums]
    pad = [jnp.zeros((16 - len(rows), 128), jnp.float32)]
    high = jnp.concatenate([h[0:1] for h, _ in rows] + pad, axis=0)
    low = jnp.concatenate([l[0:1] for _, l in rows] + pad, axis=0)
    high, low = folded(high, low, 1, (64, 32, 16, 8, 4, 2, 1))
    row = lax.broadcasted_iota(jnp.int32, (16, 128), 0)
    place = lax.broadcasted_iota(jnp.int32, (16, 128), 1)
    line = jnp.where(place == row, high, jnp.where(place == row + 16, low, 0.0))
    return jnp.broadcast_to(jnp.sum(line, axis=0, keepdims=True), (8, 128))


def no_sums():
    zero = jnp.zeros((8, 128), jnp.float32)
    return tuple((zero, zero) for _ in PAIRS)


def products(weights, source, i):
    start = i * BLOCK
    return [
        jnp.dot(
            weights[tri],
            source[start + HALF * tri : start + HALF * (tri + 3), :],
            preferred_element_type=jnp.float32,
        )
        for tri in range(2)
    ]


def bottom_planes(lanes):
    plane = lax.broadcasted_iota(jnp.int32, (24, lanes), 0)
    return (plane == 0) | (plane == 11)


def field_planes(row):
    plane = lax.broadcasted_iota(jnp.int32, (24, row.shape[1]), 0)
    return jnp.where(plane < 22, row[0:24, :], 0.0)


def diag_planes(row, theta):
    on_bottom = jnp.where(bottom_planes(row.shape[1]), row[23:24, :], 0.0)
    return row[22:23, :] * (1.0 - theta) + on_bottom


def is_inner(k, i):
    return DEPTH + k <= i <= DEPTH + 7 - k


def own_kernel(
    rhs, visc, mask, fric, stiff,
    own, packs, weights, scale, diag, powers, bounds, low_parts, high_parts,
    operand,
):
    weights_kernel(stiff, weights)
    theta = shift_of(stiff)
    lane = lax.broadcasted_iota(jnp.int32, (48, EDGE), 1)
    packed = jnp.zeros((48, EDGE), jnp.float32)
    for r in range(8):
        own_row(own.at[r], rhs, visc, mask, fric, r)
        row = own[r]
        packed = pack_row(row, r + DEPTH, lane, packed)
        put_operand(operand.at[0], r, field_planes(row))
        diag[r] = diag_planes(row, theta)
        put_scale(scale.at[r], (row[24:34, :], row[34:44, :]))
    packs[...] = packed
    for step in range(1, DEPTH + 1):
        source = operand.at[(step - 1) % 2]
        target = operand.at[step % 2]
        first, last = (step - 1, 8 - step)
        bounds[step - 1, 0] = source[first * BLOCK : (first + 1) * BLOCK, :]
        bounds[step - 1, 1] = source[last * BLOCK : (last + 1) * BLOCK, :]
        for r in range(first, last):
            a, b, c, d = grown_of(scale[r], products(weights, source, r))
            if r == first:
                low_parts[step - 1] = a + pltpu.roll(c, 1, 1)
            else:
                total = a + upper + pltpu.roll(c + across, 1, 1)
                before = powers[step - 2, r] if step > 1 else field_planes(own[r])
                x = total + diag[r] * before
                powers[step - 1, r] = x
                if step < DEPTH:
                    put_operand(target, r, x)
            upper, across = (b, d)
        high_parts[step - 1, 0] = upper
        high_parts[step - 1, 1] = across


def main_kernel(
    own, weights, own_scale, own_diag, inner, bounds, low_parts, high_parts, second_rows, first_rows, stiff,
    outer, line,
    scale, diag, field, operand,
):
    odd_row = odd_along("rx")
    theta = shift_of(stiff)
    real = {}
    for i in (0, 1, 2, 11, 12, 13):
        if i < DEPTH:
            row = jnp.where(odd_row, first_rows[i], second_rows[i])
        else:
            j = i - 8 - DEPTH
            row = jnp.where(odd_row, second_rows[j], first_rows[j])
            real[i] = row[22:23, :]
        x = field_planes(row)
        field[0, i] = x
        put_operand(operand.at[0], i, x)
        diag[i] = diag_planes(row, theta)
        if i < NROW - 1:
            put_scale(scale.at[i], (row[24:34, :], row[34:44, :]))

    def power(k, i):
        if k == 0 and is_inner(0, i):
            return field_planes(own[i - DEPTH])
        return inner[k - 1, i - DEPTH] if is_inner(k, i) else field[k, i]

    for step in range(1, DEPTH + 1):
        source = operand.at[(step - 1) % 2]
        target = operand.at[step % 2]
        for side, i in ((0, DEPTH + step - 1), (1, DEPTH + 8 - step)):
            source[i * BLOCK : (i + 1) * BLOCK, :] = bounds[step - 1, side]

        def grown(i, source=source):
            is_own = is_inner(0, i)
            return grown_of(own_scale[i - DEPTH] if is_own else scale[i], products(weights, source, i))

        def put(i, total, step=step, target=target):
            if i in real:
                total = total * real[i]
            x = total + (own_diag[i - DEPTH] if is_inner(0, i) else diag[i]) * power(step - 1, i)
            field[step, i] = x
            if is_inner(0, i):
                outer[step - 1, i - DEPTH] = x
            if step < DEPTH:
                put_operand(target, i, x)

        first = step - 1
        _, upper, _, across = grown(first)
        for i in range(first + 1, first + 3):
            a, b, c, d = grown(i)
            put(i, a + upper + pltpu.roll(c + across, 1, 1))
            upper, across = (b, d)
        put(first + 3, low_parts[step - 1] + upper + pltpu.roll(across, 1, 1))
        upper, across = (high_parts[step - 1, 0], high_parts[step - 1, 1])
        for i in range(11 - step, 14 - step):
            a, b, c, d = grown(i)
            put(i, a + upper + pltpu.roll(c + across, 1, 1))
            upper, across = (b, d)

    lane = lax.broadcasted_iota(jnp.int32, (24, LANES), 1)
    inside = (lane >= DEPTH) & (lane < LANES - DEPTH)
    sums = no_sums()
    for r in range(8):
        vectors = [jnp.where(inside, power(a, r + DEPTH), 0.0) for a in range(4)]
        sums = inner_products(vectors, sums, LANES)
    line[...] = line_of(sums)


def edge_kernel(packs, first_cols, second_cols, stiff, weights, line, edges, gram, scale):
    odd_col = odd_along("ry")
    theta = shift_of(stiff)
    at = lax.rem(lax.broadcasted_iota(jnp.int32, (48, EDGE), 1), PITCH)
    from_left = jnp.where(odd_col, first_cols[...], second_cols[...])
    from_right = jnp.where(odd_col, second_cols[...], first_cols[...])
    full = jnp.where(at < 3, from_left, jnp.where(at >= 15, from_right, packs[...]))
    put_scale(scale, (full[24:34], full[34:44]))
    real = full[22:23]
    diag = diag_planes(full, theta)
    x = field_planes(full)
    vectors = [x]
    for _ in range(DEPTH):
        corners = [
            split_rows(pltpu.roll(x, (EDGE - by) % EDGE, 1) if by else x)
            for by in (0, 1, PITCH, PITCH + 1)
        ]
        mixed = [
            jnp.dot(
                weights[tri],
                jnp.concatenate(corners[tri : tri + 3], axis=0),
                preferred_element_type=jnp.float32,
            )
            for tri in range(2)
        ]
        a, b, c, d = grown_of(scale[...], mixed)
        total = a + pltpu.roll(b, PITCH, 1) + pltpu.roll(c + pltpu.roll(d, PITCH, 1), 1, 1)
        x = real * total + diag * x
        vectors.append(x)
    for a in range(4):
        edges[a] = vectors[a]
    lane = lax.broadcasted_iota(jnp.int32, (24, EDGE), 1)
    at = lax.rem(lane, PITCH)
    mine = (lane >= PITCH * DEPTH) & (lane < PITCH * (DEPTH + 8))
    mine = mine & (((at >= 3) & (at < 6)) | ((at >= 12) & (at < 15)))
    sums = inner_products([jnp.where(mine, v, 0.0) for v in vectors], no_sums(), EDGE)
    total, rest = two_sum(line[...], line_of(sums))
    total = total + pltpu.roll(rest, 16, 1)
    gram[...] = jnp.broadcast_to(total[0:1], gram.shape)


def combine_kernel(own, inner, outer, edges, grams, stiff, update, last, parts, sems):
    theta = shift_of(stiff)
    high, low = (grams[...], jnp.zeros(grams.shape, jnp.float32))
    while high.shape[0] > 8 and high.shape[0] % 16 == 0:
        half = high.shape[0] // 2
        high, rest = two_sum(high[:half], high[half:])
        low = low[:half] + low[half:] + rest
    for start in range(8, high.shape[0], 8):
        total, rest = two_sum(high[0:8], high[start : start + 8])
        high = jnp.concatenate([total, high[8:]], axis=0)
        low = jnp.concatenate([low[0:8] + low[start : start + 8] + rest, low[8:]], axis=0)
    if high.shape[0] >= 8:
        high, low = folded(high[0:8], low[0:8], 0, (4, 2, 1))
    else:
        high, low = (jnp.sum(high, axis=0, keepdims=True), jnp.sum(low, axis=0, keepdims=True))
    high, low = (high[0:1], low[0:1])
    place = lax.broadcasted_iota(jnp.int32, (1, 128), 1)

    def lane_of(line, n):
        return jnp.sum(jnp.where(place == n, line, 0.0), axis=1, keepdims=True)

    g = {}
    for n, pair in enumerate(PAIRS):
        g[pair] = pair_of(lane_of(high, n), lane_of(high, n + 16) + lane_of(low, n))
    upper = [[None] * 4 for _ in range(4)]
    inverse = [None] * 4
    for a in range(4):
        inverse[a] = lax.rsqrt(g[a, a][0])
        upper[a][a] = g[a, a][0] * inverse[a]
        for b in range(a + 1, 4):
            upper[a][b] = g[a, b][0] * inverse[a]
        for b in range(a + 1, 4):
            ratio = pair_over(g[a, b], g[a, a])
            for c in range(b, 4):
                g[b, c] = pair_less(g[b, c], pair_times(ratio, g[a, c]))
    zero = jnp.zeros((1, 1), jnp.float32)
    table = [
        [
            (upper[a][b + 1] if a <= b + 1 else zero) + (theta * upper[a][b] if a <= b else zero)
            for b in range(3)
        ]
        for a in range(4)
    ]
    target = [upper[0][0], zero, zero, zero]
    turned = [None] * 3
    for col in range(3):
        first, second = (table[col][col], table[col + 1][col])
        turned[col] = lax.rsqrt(first * first + second * second)
        cosine, sine = (first * turned[col], second * turned[col])
        for c in range(col, 3):
            one, two = (table[col][c], table[col + 1][c])
            table[col][c] = cosine * one + sine * two
            table[col + 1][c] = cosine * two - sine * one
        one, two = (target[col], target[col + 1])
        target[col] = cosine * one + sine * two
        target[col + 1] = cosine * two - sine * one
    z = [None] * 3
    for col in (2, 1, 0):
        value = target[col]
        for c in range(col + 1, 3):
            value = value - table[col][c] * z[c]
        z[col] = value * turned[col]
    w = [None] * 4
    w[3] = inverse[3]
    for a in (2, 1, 0):
        value = zero
        for c in range(a + 1, 4):
            value = value - upper[a][c] * w[c]
        w[a] = value * inverse[a]
    lane = lax.broadcasted_iota(jnp.int32, (8, 128), 1)
    copies = []
    for n, (out, factors) in enumerate(((update, z), (last, w))):
        ends = factors[0] * edges[0]
        for a in range(1, len(factors)):
            ends = ends + factors[a] * edges[a]
        for g, planes in enumerate((slice(0, 8), slice(8, 16), slice(16, 22))):
            count = planes.stop - planes.start
            for r in range(8):
                row = factors[0] * own[r, planes, :]
                for a in range(1, len(factors)):
                    part = inner if is_inner(a, r + DEPTH) else outer
                    row = row + factors[a] * part[a - 1, r, planes, :]
                at = PITCH * (r + DEPTH)
                left = pltpu.roll(ends[planes], (EDGE - at - 3) % EDGE, 1)[:, 0:128]
                right = pltpu.roll(ends[planes], (253 - at - 12) % EDGE, 1)[:, 128:256]
                inside = lane[0:count]
                parts[n, planes, r, 0:128] = jnp.where(inside < DEPTH, left, row[:, 0:128])
                parts[n, planes, r, 128:384] = row[:, 128:384]
                parts[n, planes, r, 384:512] = jnp.where(
                    inside >= 128 - DEPTH, right, row[:, 384:512]
                )
            copies.append(
                pltpu.make_async_copy(parts.at[n, planes], out.at[planes], sems.at[3 * n + g])
            )
            copies[-1].start()
    for copy in copies:
        copy.wait()


def call(kernel, outs, scratch=(), flops=0, bytes_accessed=0, limit=8, in_hbm=0, out_hbm=0):
    single = not isinstance(outs, (list, tuple))
    extra = {"in_specs": [pl.BlockSpec(memory_space=pltpu.HBM)] * in_hbm} if in_hbm else {}
    if out_hbm:
        extra["out_specs"] = (pl.BlockSpec(memory_space=pltpu.HBM),) * out_hbm
    return pl.pallas_call(
        kernel,
        out_shape=outs if single else tuple(outs),
        scratch_shapes=list(scratch),
        **extra,
        compiler_params=pltpu.CompilerParams(vmem_limit_bytes=limit * 1024 * 1024),
        cost_estimate=pl.CostEstimate(
            flops=flops, bytes_accessed=bytes_accessed, transcendentals=0
        ),
    )


def f32(*shape):
    return jax.ShapeDtypeStruct(shape, jnp.float32)


def swapped(shard, axis, start):
    pairs = []
    for i in range(start, lax.axis_size(axis) - 1, 2):
        pairs += [(i, i + 1), (i + 1, i)]
    return lax.ppermute(shard, axis, pairs)


def body(rhs, viscosity, cell_mask, friction, stiffness):
    devices = lax.axis_size("rx") * lax.axis_size("ry")
    natural = [
        pltpu.with_memory_space_constraint(x, pltpu.HBM)
        for x in (rhs.reshape(22, 8, 512), viscosity, cell_mask, friction, stiffness.transpose(1, 0, 2))
    ]
    first, second, *local, stiff = call(
        rows_kernel,
        (f32(DEPTH, 48, 512), f32(DEPTH, 48, 512), f32(22, 8, 512), f32(10, 2, 8, 512),
         jax.ShapeDtypeStruct((8, 512), jnp.int32), f32(8, 512), f32(12, 2, 12)),
        [pltpu.VMEM((2, 48, 512), jnp.float32), pltpu.SemaphoreType.DMA((5,))],
        bytes_accessed=10**6,
        in_hbm=5,
    )(*natural)
    first_rows = swapped(first, "rx", 0)
    second_rows = swapped(second, "rx", 1)
    own, packs, weights, *prepared = call(
        own_kernel,
        (
            f32(8, 48, LANES),
            f32(48, EDGE),
            jax.ShapeDtypeStruct((2, GROUPS, 3 * HALF), jnp.bfloat16),
            f32(8, 96, LANES),
            f32(8, 24, LANES),
            f32(3, 8, 24, LANES),
            jax.ShapeDtypeStruct((3, 2, BLOCK, LANES), jnp.bfloat16),
            f32(3, 24, LANES),
            f32(3, 2, 24, LANES),
        ),
        [pltpu.VMEM((2, 8 * BLOCK, LANES), jnp.bfloat16)],
        flops=10**9,
        bytes_accessed=10**6,
        limit=16,
    )(*local, stiff)
    inner = prepared[2]
    packs = call(cols_kernel, f32(48, EDGE), bytes_accessed=10**6)(packs, second_rows, first_rows)
    first_cols = swapped(packs, "ry", 0)
    second_cols = swapped(packs, "ry", 1)
    outer, line = call(
        main_kernel,
        (f32(3, 8, 24, LANES), f32(8, 128)),
        [
            pltpu.VMEM((NROW - 1, 96, LANES), jnp.float32),
            pltpu.VMEM((NROW, 24, LANES), jnp.float32),
            pltpu.VMEM((4, NROW, 24, LANES), jnp.float32),
            pltpu.VMEM((2, NROW * BLOCK, LANES), jnp.bfloat16),
        ],
        flops=2 * 10**9,
        bytes_accessed=3 * 10**6,
        limit=24,
    )(own, weights, *prepared, second_rows, first_rows, stiff)
    edges, gram = call(
        edge_kernel,
        (f32(4, 24, EDGE), f32(devices, 128)),
        [pltpu.VMEM((96, EDGE), jnp.float32)],
        flops=10**8,
        bytes_accessed=10**6,
    )(packs, first_cols, second_cols, stiff, weights, line)
    grams = lax.all_to_all(gram.reshape(devices, 1, 128), ("rx", "ry"), 0, 0)
    update, last = call(
        combine_kernel,
        (f32(22, 8, 512),) * 2,
        [pltpu.VMEM((2, 22, 8, 512), jnp.float32), pltpu.SemaphoreType.DMA((6,))],
        bytes_accessed=3 * 10**6,
        out_hbm=2,
    )(
        own, inner, outer, edges, grams.reshape(devices, 128), stiff
    )
    return update.reshape(2, 11, 8, 512), last.reshape(2, 11, 8, 512)


def solution(mesh):
    in_specs = (
        P(None, None, "rx", "ry"),
        P(None, None, "rx", "ry"),
        P("rx", "ry"),
        P("rx", "ry"),
        P(),
    )
    out_specs = (P(None, None, "rx", "ry"), P(None, None, "rx", "ry"))
    return jax.shard_map(body, mesh=mesh, in_specs=in_specs, out_specs=out_specs, check_vma=False)
```

```python
import jax
import jax.numpy as jnp
from jax import lax
from jax.experimental import pallas as pl
from jax.experimental.pallas import tpu as pltpu
from jax.sharding import PartitionSpec as P


DEPTH = 3
NROW = 8 + 2 * DEPTH
LANES = 512
PITCH = 18
EDGE = 256
PAIRS = [(a, b) for a in range(4) for b in range(a, 4)]
HALF = 80
BLOCK = 2 * HALF
GROUPS = 144


def shift_of(stiff):
    rows = lax.broadcasted_iota(jnp.int32, (12, 12), 0)
    cols = lax.broadcasted_iota(jnp.int32, (12, 12), 1)
    trace = jnp.sum(jnp.where(rows == cols, stiff[:, 0, :] + stiff[:, 1, :], 0.0))
    return 1.0 + trace * (1.2 * 10.0 / 22.0)


def own_row(out, rhs, visc, mask, fric, row):
    ice = mask[row : row + 1, :].astype(jnp.float32)
    out[0:22, 0:512] = rhs[:, row, :]
    out[22:23, 0:512] = jnp.ones_like(ice)
    out[23:24, 0:512] = fric[row : row + 1, :]
    out[24:34, 0:512] = visc[:, 0, row, :] * ice
    out[34:44, 0:512] = visc[:, 1, row, :] * ice
    out[44:48, 0:512] = jnp.zeros((4, 512), jnp.float32)


def odd_along(axis):
    return lax.rem(lax.axis_index(axis), 2) == 1


def rows_kernel(
    rhs, visc, mask, fric, stiff,
    first, second, rhs_out, visc_out, mask_out, fric_out, stiff_out,
    work, sems,
):
    sources = (rhs, visc, mask, fric, stiff)
    targets = (rhs_out, visc_out, mask_out, fric_out, stiff_out)
    copies = [
        pltpu.make_async_copy(src, dst, sems.at[n])
        for n, (src, dst) in enumerate(zip(sources, targets))
    ]
    for copy in copies:
        copy.start()
    for copy in copies:
        copy.wait()
    odd = odd_along("rx")
    for j in range(DEPTH):
        own_row(work.at[0], rhs_out, visc_out, mask_out, fric_out, 8 - DEPTH + j)
        own_row(work.at[1], rhs_out, visc_out, mask_out, fric_out, j)
        up, down = (work[0], work[1])
        first[j] = jnp.where(odd, down, up)
        second[j] = jnp.where(odd, up, down)


def pack_row(row, i, lane, packed):
    ends = jnp.concatenate([row[:, 0:128], row[:, 384:512]], axis=1)
    at = lane - PITCH * i
    packed = jnp.where((at >= 0) & (at < 9), pltpu.roll(ends, (PITCH * i + 3) % EDGE, 1), packed)
    return jnp.where((at >= 9) & (at < 18), pltpu.roll(ends, (PITCH * i + 15) % EDGE, 1), packed)


def cols_kernel(packs, second_rows, first_rows, out):
    odd_row = odd_along("rx")
    lane = lax.broadcasted_iota(jnp.int32, (48, 128), 1)
    halves = [packs[:, 0:128], packs[:, 128:256]]
    for j in range(DEPTH):
        one, two = [
            jnp.where(lane < 64, rows[j, :, 0:128], rows[j, :, 384:512])
            for rows in (first_rows, second_rows)
        ]
        low, high = (jnp.where(odd_row, one, two), jnp.where(odd_row, two, one))
        for half, row, i in ((0, low, j), (1, high, j + 8 + DEPTH)):
            start = PITCH * i - 128 * half
            at = lane - start
            packed = jnp.where((at >= 0) & (at < 9), pltpu.roll(row, start + 3, 1), halves[half])
            halves[half] = jnp.where(
                (at >= 9) & (at < 18), pltpu.roll(row, (start + 15) % 128, 1), packed
            )
    out[:, 0:128] = halves[0]
    out[:, 128:256] = halves[1]


def weights_kernel(stiff, weights):
    row = lax.broadcasted_iota(jnp.int32, (GROUPS, 12), 0)
    col = lax.broadcasted_iota(jnp.int32, (GROUPS, 12), 1)

    def of_row(r):
        group, plane = (r // 24, r % 24)
        slot, lev = (group // 2, group % 2)
        comp, level = (plane // 11, plane % 11)
        layer = level - lev
        good = (plane < 22) & (layer >= 0) & (layer < 10)
        return comp * 6 + lev * 3 + slot, layer, good

    pick = jnp.where(of_row(row)[0] == col, 1.0, 0.0)
    r = lax.broadcasted_iota(jnp.int32, (GROUPS, 3 * HALF), 0)
    k = lax.broadcasted_iota(jnp.int32, (GROUPS, 3 * HALF), 1)
    _, layer, good = of_row(r)
    part = (k % HALF) // 24
    plane = (k % HALF) % 24
    lev_in = plane % 11 - layer
    good = good & (part < 3) & (plane < 22)
    q = lax.broadcasted_iota(jnp.int32, (12, 3 * HALF), 0)
    kq = lax.broadcasted_iota(jnp.int32, (12, 3 * HALF), 1)
    comp_in = ((kq % HALF) % 24) // 11
    block = kq // HALF
    for tri in range(2):
        first, second, third = ((0, 2, 1), (2, 0, 1))[tri]
        place = jnp.where(block == 0, first, jnp.where(block == 1, second, third))
        rows = jnp.dot(
            pick, stiff[:, tri, :], precision=lax.Precision.HIGHEST, preferred_element_type=jnp.float32
        )
        total = jnp.zeros((GROUPS, 3 * HALF), jnp.float32)
        for lev in range(2):
            sel = jnp.where(comp_in * 6 + lev * 3 + place == q, 1.0, 0.0)
            spread = jnp.dot(
                rows, sel, precision=lax.Precision.HIGHEST, preferred_element_type=jnp.float32
            )
            total = jnp.where(good & (lev_in == lev), spread, total)
        high = total.astype(jnp.bfloat16).astype(jnp.float32)
        weights[tri] = jnp.where(part == 2, total - high, high).astype(jnp.bfloat16)


def split_rows(x):
    high = x.astype(jnp.bfloat16).astype(jnp.float32)
    pad = jnp.zeros((HALF - 72, x.shape[1]), jnp.float32)
    return jnp.concatenate([high, x - high, high, pad], axis=0).astype(jnp.bfloat16)


def put_operand(operand, i, x):
    operand[i * BLOCK : i * BLOCK + HALF, :] = split_rows(x)
    operand[i * BLOCK + HALF : (i + 1) * BLOCK, :] = split_rows(pltpu.roll(x, LANES - 1, 1))


def put_scale(out, coefs):
    zeros = jnp.zeros((24, out.shape[1]), jnp.float32)
    for tri in range(2):
        for lev in range(2):
            base = 48 * tri + 24 * lev
            out[base : base + 24, :] = zeros
            out[base + lev : base + lev + 10, :] = coefs[tri]
            out[base + 11 + lev : base + 21 + lev, :] = coefs[tri]


def grown_of(scale, mixed):
    parts = []
    for tri in range(2):
        upper = scale[48 * tri : 48 * tri + 24, :]
        lower = scale[48 * tri + 24 : 48 * tri + 48, :]
        for slot in range(3):
            at = 48 * slot
            parts.append(upper * mixed[tri][at : at + 24] + lower * mixed[tri][at + 24 : at + 48])
    return parts[0], parts[1] + parts[3], parts[2] + parts[5], parts[4]


def inner_products(vectors, sums, lanes):
    result = []
    for total, (a, b) in zip(sums, PAIRS):
        product = vectors[a] * vectors[b]
        terms = [
            product[s : s + 8, l : l + 128] for s in range(0, 24, 8) for l in range(0, lanes, 128)
        ]
        while len(terms) > 1:
            terms = [sum(terms[n : n + 2][1:], terms[n]) for n in range(0, len(terms), 2)]
        result.append(total + terms[0])
    return tuple(result)


def line_of(sums):
    rows = [jnp.sum(total, axis=0, keepdims=True) for total in sums]
    rows.append(jnp.zeros((16 - len(rows), 128), jnp.float32))
    totals = jnp.sum(jnp.concatenate(rows, axis=0), axis=1, keepdims=True)
    row = lax.broadcasted_iota(jnp.int32, (16, 128), 0)
    place = lax.broadcasted_iota(jnp.int32, (16, 128), 1)
    line = jnp.sum(jnp.where(place == row, totals, 0.0), axis=0, keepdims=True)
    return jnp.broadcast_to(line, (8, 128))


def no_sums():
    return tuple(jnp.zeros((8, 128), jnp.float32) for _ in PAIRS)


def products(weights, source, i):
    start = i * BLOCK
    return [
        jnp.dot(
            weights[tri],
            source[start + HALF * tri : start + HALF * (tri + 3), :],
            preferred_element_type=jnp.float32,
        )
        for tri in range(2)
    ]


def bottom_planes(lanes):
    plane = lax.broadcasted_iota(jnp.int32, (24, lanes), 0)
    return (plane == 0) | (plane == 11)


def field_planes(row):
    plane = lax.broadcasted_iota(jnp.int32, (24, row.shape[1]), 0)
    return jnp.where(plane < 22, row[0:24, :], 0.0)


def diag_planes(row, theta):
    on_bottom = jnp.where(bottom_planes(row.shape[1]), row[23:24, :], 0.0)
    return row[22:23, :] * (1.0 - theta) + on_bottom


def is_inner(k, i):
    return DEPTH + k <= i <= DEPTH + 7 - k


def own_kernel(
    rhs, visc, mask, fric, stiff,
    own, packs, weights, scale, diag, powers, bounds, low_parts, high_parts,
    operand,
):
    weights_kernel(stiff, weights)
    theta = shift_of(stiff)
    lane = lax.broadcasted_iota(jnp.int32, (48, EDGE), 1)
    packed = jnp.zeros((48, EDGE), jnp.float32)
    for r in range(8):
        own_row(own.at[r], rhs, visc, mask, fric, r)
        row = own[r]
        packed = pack_row(row, r + DEPTH, lane, packed)
        put_operand(operand.at[0], r, field_planes(row))
        diag[r] = diag_planes(row, theta)
        put_scale(scale.at[r], (row[24:34, :], row[34:44, :]))
    packs[...] = packed
    for step in range(1, DEPTH + 1):
        source = operand.at[(step - 1) % 2]
        target = operand.at[step % 2]
        first, last = (step - 1, 8 - step)
        bounds[step - 1, 0] = source[first * BLOCK : (first + 1) * BLOCK, :]
        bounds[step - 1, 1] = source[last * BLOCK : (last + 1) * BLOCK, :]
        for r in range(first, last):
            a, b, c, d = grown_of(scale[r], products(weights, source, r))
            if r == first:
                low_parts[step - 1] = a + pltpu.roll(c, 1, 1)
            else:
                total = a + upper + pltpu.roll(c + across, 1, 1)
                before = powers[step - 2, r] if step > 1 else field_planes(own[r])
                x = total + diag[r] * before
                powers[step - 1, r] = x
                if step < DEPTH:
                    put_operand(target, r, x)
            upper, across = (b, d)
        high_parts[step - 1, 0] = upper
        high_parts[step - 1, 1] = across


def main_kernel(
    own, weights, own_scale, own_diag, inner, bounds, low_parts, high_parts, second_rows, first_rows, stiff,
    outer, line,
    scale, diag, field, operand,
):
    odd_row = odd_along("rx")
    theta = shift_of(stiff)
    real = {}
    for i in (0, 1, 2, 11, 12, 13):
        if i < DEPTH:
            row = jnp.where(odd_row, first_rows[i], second_rows[i])
        else:
            j = i - 8 - DEPTH
            row = jnp.where(odd_row, second_rows[j], first_rows[j])
            real[i] = row[22:23, :]
        x = field_planes(row)
        field[0, i] = x
        put_operand(operand.at[0], i, x)
        diag[i] = diag_planes(row, theta)
        if i < NROW - 1:
            put_scale(scale.at[i], (row[24:34, :], row[34:44, :]))

    def power(k, i):
        if k == 0 and is_inner(0, i):
            return field_planes(own[i - DEPTH])
        return inner[k - 1, i - DEPTH] if is_inner(k, i) else field[k, i]

    for step in range(1, DEPTH + 1):
        source = operand.at[(step - 1) % 2]
        target = operand.at[step % 2]
        for side, i in ((0, DEPTH + step - 1), (1, DEPTH + 8 - step)):
            source[i * BLOCK : (i + 1) * BLOCK, :] = bounds[step - 1, side]

        def grown(i, source=source):
            is_own = is_inner(0, i)
            return grown_of(own_scale[i - DEPTH] if is_own else scale[i], products(weights, source, i))

        def put(i, total, step=step, target=target):
            if i in real:
                total = total * real[i]
            x = total + (own_diag[i - DEPTH] if is_inner(0, i) else diag[i]) * power(step - 1, i)
            field[step, i] = x
            if is_inner(0, i):
                outer[step - 1, i - DEPTH] = x
            if step < DEPTH:
                put_operand(target, i, x)

        first = step - 1
        _, upper, _, across = grown(first)
        for i in range(first + 1, first + 3):
            a, b, c, d = grown(i)
            put(i, a + upper + pltpu.roll(c + across, 1, 1))
            upper, across = (b, d)
        put(first + 3, low_parts[step - 1] + upper + pltpu.roll(across, 1, 1))
        upper, across = (high_parts[step - 1, 0], high_parts[step - 1, 1])
        for i in range(11 - step, 14 - step):
            a, b, c, d = grown(i)
            put(i, a + upper + pltpu.roll(c + across, 1, 1))
            upper, across = (b, d)

    lane = lax.broadcasted_iota(jnp.int32, (24, LANES), 1)
    inside = (lane >= DEPTH) & (lane < LANES - DEPTH)
    sums = no_sums()
    for r in range(8):
        vectors = [jnp.where(inside, power(a, r + DEPTH), 0.0) for a in range(4)]
        sums = inner_products(vectors, sums, LANES)
    line[...] = line_of(sums)


def edge_kernel(packs, first_cols, second_cols, stiff, weights, line, edges, gram, scale):
    odd_col = odd_along("ry")
    theta = shift_of(stiff)
    at = lax.rem(lax.broadcasted_iota(jnp.int32, (48, EDGE), 1), PITCH)
    from_left = jnp.where(odd_col, first_cols[...], second_cols[...])
    from_right = jnp.where(odd_col, second_cols[...], first_cols[...])
    full = jnp.where(at < 3, from_left, jnp.where(at >= 15, from_right, packs[...]))
    put_scale(scale, (full[24:34], full[34:44]))
    real = full[22:23]
    diag = diag_planes(full, theta)
    x = field_planes(full)
    vectors = [x]
    for _ in range(DEPTH):
        corners = [
            split_rows(pltpu.roll(x, (EDGE - by) % EDGE, 1) if by else x)
            for by in (0, 1, PITCH, PITCH + 1)
        ]
        mixed = [
            jnp.dot(
                weights[tri],
                jnp.concatenate(corners[tri : tri + 3], axis=0),
                preferred_element_type=jnp.float32,
            )
            for tri in range(2)
        ]
        a, b, c, d = grown_of(scale[...], mixed)
        total = a + pltpu.roll(b, PITCH, 1) + pltpu.roll(c + pltpu.roll(d, PITCH, 1), 1, 1)
        x = real * total + diag * x
        vectors.append(x)
    for a in range(4):
        edges[a] = vectors[a]
    lane = lax.broadcasted_iota(jnp.int32, (24, EDGE), 1)
    at = lax.rem(lane, PITCH)
    mine = (lane >= PITCH * DEPTH) & (lane < PITCH * (DEPTH + 8))
    mine = mine & (((at >= 3) & (at < 6)) | ((at >= 12) & (at < 15)))
    sums = inner_products([jnp.where(mine, v, 0.0) for v in vectors], no_sums(), EDGE)
    total = line[...] + line_of(sums)
    gram[...] = jnp.broadcast_to(total[0:1], gram.shape)


def combine_kernel(own, inner, outer, edges, grams, stiff, update, last, parts, sems):
    theta = shift_of(stiff)
    entry = jnp.sum(grams[...], axis=0, keepdims=True)
    place = lax.broadcasted_iota(jnp.int32, (1, 128), 1)
    g = {}
    for n, pair in enumerate(PAIRS):
        g[pair] = jnp.sum(jnp.where(place == n, entry, 0.0), axis=1, keepdims=True)
    upper = [[None] * 4 for _ in range(4)]
    inverse = [None] * 4
    for a in range(4):
        for b in range(a, 4):
            value = g[a, b]
            for c in range(a):
                value = value - upper[c][a] * upper[c][b]
            if a == b:
                inverse[a] = lax.rsqrt(value)
                upper[a][a] = value * inverse[a]
            else:
                upper[a][b] = value * inverse[a]
    zero = jnp.zeros((1, 1), jnp.float32)
    table = [
        [
            (upper[a][b + 1] if a <= b + 1 else zero) + (theta * upper[a][b] if a <= b else zero)
            for b in range(3)
        ]
        for a in range(4)
    ]
    target = [upper[0][0], zero, zero, zero]
    turned = [None] * 3
    for col in range(3):
        first, second = (table[col][col], table[col + 1][col])
        turned[col] = lax.rsqrt(first * first + second * second)
        cosine, sine = (first * turned[col], second * turned[col])
        for c in range(col, 3):
            one, two = (table[col][c], table[col + 1][c])
            table[col][c] = cosine * one + sine * two
            table[col + 1][c] = cosine * two - sine * one
        one, two = (target[col], target[col + 1])
        target[col] = cosine * one + sine * two
        target[col + 1] = cosine * two - sine * one
    z = [None] * 3
    for col in (2, 1, 0):
        value = target[col]
        for c in range(col + 1, 3):
            value = value - table[col][c] * z[c]
        z[col] = value * turned[col]
    w = [None] * 4
    w[3] = inverse[3]
    for a in (2, 1, 0):
        value = zero
        for c in range(a + 1, 4):
            value = value - upper[a][c] * w[c]
        w[a] = value * inverse[a]
    lane = lax.broadcasted_iota(jnp.int32, (8, 128), 1)
    copies = []
    for n, (out, factors) in enumerate(((update, z), (last, w))):
        ends = factors[0] * edges[0]
        for a in range(1, len(factors)):
            ends = ends + factors[a] * edges[a]
        for g, planes in enumerate((slice(0, 8), slice(8, 16), slice(16, 22))):
            count = planes.stop - planes.start
            for r in range(8):
                row = factors[0] * own[r, planes, :]
                for a in range(1, len(factors)):
                    part = inner if is_inner(a, r + DEPTH) else outer
                    row = row + factors[a] * part[a - 1, r, planes, :]
                at = PITCH * (r + DEPTH)
                left = pltpu.roll(ends[planes], (EDGE - at - 3) % EDGE, 1)[:, 0:128]
                right = pltpu.roll(ends[planes], (253 - at - 12) % EDGE, 1)[:, 128:256]
                inside = lane[0:count]
                parts[n, planes, r, 0:128] = jnp.where(inside < DEPTH, left, row[:, 0:128])
                parts[n, planes, r, 128:384] = row[:, 128:384]
                parts[n, planes, r, 384:512] = jnp.where(
                    inside >= 128 - DEPTH, right, row[:, 384:512]
                )
            copies.append(
                pltpu.make_async_copy(parts.at[n, planes], out.at[planes], sems.at[3 * n + g])
            )
            copies[-1].start()
    for copy in copies:
        copy.wait()


def call(kernel, outs, scratch=(), flops=0, bytes_accessed=0, limit=8, in_hbm=0, out_hbm=0):
    single = not isinstance(outs, (list, tuple))
    extra = {"in_specs": [pl.BlockSpec(memory_space=pltpu.HBM)] * in_hbm} if in_hbm else {}
    if out_hbm:
        extra["out_specs"] = (pl.BlockSpec(memory_space=pltpu.HBM),) * out_hbm
    return pl.pallas_call(
        kernel,
        out_shape=outs if single else tuple(outs),
        scratch_shapes=list(scratch),
        **extra,
        compiler_params=pltpu.CompilerParams(vmem_limit_bytes=limit * 1024 * 1024),
        cost_estimate=pl.CostEstimate(
            flops=flops, bytes_accessed=bytes_accessed, transcendentals=0
        ),
    )


def f32(*shape):
    return jax.ShapeDtypeStruct(shape, jnp.float32)


def swapped(shard, axis, start):
    pairs = []
    for i in range(start, lax.axis_size(axis) - 1, 2):
        pairs += [(i, i + 1), (i + 1, i)]
    return lax.ppermute(shard, axis, pairs)


def body(rhs, viscosity, cell_mask, friction, stiffness):
    devices = lax.axis_size("rx") * lax.axis_size("ry")
    natural = [
        pltpu.with_memory_space_constraint(x, pltpu.HBM)
        for x in (rhs.reshape(22, 8, 512), viscosity, cell_mask, friction, stiffness.transpose(1, 0, 2))
    ]
    first, second, *local, stiff = call(
        rows_kernel,
        (f32(DEPTH, 48, 512), f32(DEPTH, 48, 512), f32(22, 8, 512), f32(10, 2, 8, 512),
         jax.ShapeDtypeStruct((8, 512), jnp.int32), f32(8, 512), f32(12, 2, 12)),
        [pltpu.VMEM((2, 48, 512), jnp.float32), pltpu.SemaphoreType.DMA((5,))],
        bytes_accessed=10**6,
        in_hbm=5,
    )(*natural)
    first_rows = swapped(first, "rx", 0)
    second_rows = swapped(second, "rx", 1)
    own, packs, weights, *prepared = call(
        own_kernel,
        (
            f32(8, 48, LANES),
            f32(48, EDGE),
            jax.ShapeDtypeStruct((2, GROUPS, 3 * HALF), jnp.bfloat16),
            f32(8, 96, LANES),
            f32(8, 24, LANES),
            f32(3, 8, 24, LANES),
            jax.ShapeDtypeStruct((3, 2, BLOCK, LANES), jnp.bfloat16),
            f32(3, 24, LANES),
            f32(3, 2, 24, LANES),
        ),
        [pltpu.VMEM((2, 8 * BLOCK, LANES), jnp.bfloat16)],
        flops=10**9,
        bytes_accessed=10**6,
        limit=16,
    )(*local, stiff)
    inner = prepared[2]
    packs = call(cols_kernel, f32(48, EDGE), bytes_accessed=10**6)(packs, second_rows, first_rows)
    first_cols = swapped(packs, "ry", 0)
    second_cols = swapped(packs, "ry", 1)
    outer, line = call(
        main_kernel,
        (f32(3, 8, 24, LANES), f32(8, 128)),
        [
            pltpu.VMEM((NROW - 1, 96, LANES), jnp.float32),
            pltpu.VMEM((NROW, 24, LANES), jnp.float32),
            pltpu.VMEM((4, NROW, 24, LANES), jnp.float32),
            pltpu.VMEM((2, NROW * BLOCK, LANES), jnp.bfloat16),
        ],
        flops=2 * 10**9,
        bytes_accessed=3 * 10**6,
        limit=24,
    )(own, weights, *prepared, second_rows, first_rows, stiff)
    edges, gram = call(
        edge_kernel,
        (f32(4, 24, EDGE), f32(devices, 128)),
        [pltpu.VMEM((96, EDGE), jnp.float32)],
        flops=10**8,
        bytes_accessed=10**6,
    )(packs, first_cols, second_cols, stiff, weights, line)
    grams = lax.all_to_all(gram.reshape(devices, 1, 128), ("rx", "ry"), 0, 0)
    update, last = call(
        combine_kernel,
        (f32(22, 8, 512),) * 2,
        [pltpu.VMEM((2, 22, 8, 512), jnp.float32), pltpu.SemaphoreType.DMA((6,))],
        bytes_accessed=3 * 10**6,
        out_hbm=2,
    )(
        own, inner, outer, edges, grams.reshape(devices, 128), stiff
    )
    return update.reshape(2, 11, 8, 512), last.reshape(2, 11, 8, 512)


def solution(mesh):
    in_specs = (
        P(None, None, "rx", "ry"),
        P(None, None, "rx", "ry"),
        P("rx", "ry"),
        P("rx", "ry"),
        P(),
    )
    out_specs = (P(None, None, "rx", "ry"), P(None, None, "rx", "ry"))
    return jax.shard_map(body, mesh=mesh, in_specs=in_specs, out_specs=out_specs, check_vma=False)
```
